512 devices in a mesh: outer: 8 (over z_lo, core), dev: 64 (over x, z_hi, y).
Axes of the slice: x: 4, y: 8, z: 8 (z_hi: 2, z_lo: 4; z = z_hi * 4 + z_lo), core: 2. Of those that a mesh axis runs over, the one named last changes fastest.
Arguments:
- pseudo_grad: float32 [8, 8192, 256], P('outer', 'dev'), may hold values from -6 to 6
- grad_expo: int32 [8, 8192], P('outer', 'dev'), may hold values from -2 to 2
- sign_bits: int32 [8192, 256], P('dev'), may hold values from 0 to 1
- params: float32 [8192, 256], P(('dev', 'outer')), may hold values from -6 to 6
- momentum: float32 [8192, 256], P(('dev', 'outer')), may hold values from -6 to 6
- param_expo: int32 [8192], P(('dev', 'outer')), may hold values from -2 to 2
Outputs:
- new_params: float32 [8192, 256], P(('dev', 'outer'))
- new_momentum: float32 [8192, 256], P(('dev', 'outer'))
- fragment_codes: bfloat16 [8192, 256], replicated
The draws below stay inside these ranges and needn't reach their ends.
Inputs may be any that keep to these rules, and one draw needn't show every extreme that they name: `sign_bits`: 0 stands for the sign -1 and 1 for +1.
All inputs are finite; a program needn't handle non-finite values.
Results may differ from the reference program's by a relative error of at most 0.0085.
Values may be sent and summed in bfloat16 or wider, within the bound.
No kernel may reach another device: no remote copies, remote signals or barrier semaphores. Data moves between devices by JAX's collectives and lax.ppermute only.
A program may use at most 64 MiB of HBM per device.

```python
import jax
import jax.numpy as jnp
from jax import lax

HB = 256
BLOCKS = 8192
REPLICAS = 8


def place_ends(array, key, least, high):
    dims = array.shape
    spot = [jax.random.randint(jax.random.fold_in(key, axis), (), 0, dims[axis]) for axis in range(len(dims))]
    array = array.at[tuple(spot)].set(least)
    longest = dims.index(max(dims))
    spot[longest] = (spot[longest] + 1) % dims[longest]
    return array.at[tuple(spot)].set(high)


def levels(key, shape, shards, smallest, high):
    loudness, own = 1.0, jax.random.fold_in(key, 6)
    for dim, shards_of in shards:
        draws = jnp.exp(jax.random.uniform(jax.random.fold_in(own, dim), (shards_of,), jnp.float32, smallest / len(shards), high / len(shards)))
        loudness = loudness * jnp.repeat(draws, shape[dim] // shards_of).reshape([-1 if axis == dim else 1 for axis in range(len(shape))])
    return loudness


def scatter_about(stream_key, shape, scale, most, split=(), kind=jnp.bfloat16):
    loudness = levels(stream_key, shape, split, -0.22, 0.18) if split else 1.0
    values = jax.random.normal(stream_key, shape, jnp.float32) * scale * loudness
    return jnp.minimum(jnp.maximum(values, -most), most).astype(kind)


def setup_inputs(seed: int = 0) -> dict:
    key_list = jax.random.split(jax.random.key(seed), 7)
    return {
        "pseudo_grad": scatter_about(key_list[0], (REPLICAS, BLOCKS, HB), 1.0, 6.0, ((0, 8), (1, 64)), jnp.float32),
        "grad_expo": place_ends(jax.random.randint(key_list[1], (REPLICAS, BLOCKS), -2, 3), jax.random.fold_in(key_list[1], 1), -2, 2).astype(jnp.int32),
        "sign_bits": place_ends(jax.random.randint(key_list[2], (BLOCKS, HB), 0, 2), jax.random.fold_in(key_list[2], 1), 0, 1).astype(jnp.int32),
        "params": scatter_about(key_list[3], (BLOCKS, HB), 1.0, 6.0, ((0, 512),), jnp.float32),
        "momentum": scatter_about(key_list[4], (BLOCKS, HB), 0.7, 6.0, ((0, 512),), jnp.float32),
        "param_expo": place_ends(jax.random.randint(key_list[5], (BLOCKS,), -2, 3), jax.random.fold_in(key_list[5], 1), -2, 2).astype(jnp.int32),
    }


def hadamard(width):
    index = jnp.arange(width, dtype=jnp.int32)
    common = index[:, None] & index[None, :]
    parity = jnp.zeros((width, width), jnp.int32)
    for bit in range(width.bit_length() - 1):
        parity = parity + (common >> bit & 1)
    return (1 - 2 * (parity % 2)).astype(jnp.float32)

def reference(pseudo_grad, grad_expo, sign_bits, params, momentum, param_expo):
    table = hadamard(HB)
    inv_root = 1.0 / jnp.sqrt(jnp.float32(HB))
    sign = (2 * sign_bits - 1).astype(jnp.float32)
    rotated = jnp.einsum('rbi,ij->rbj', pseudo_grad * sign[None], table, precision=lax.Precision.HIGHEST) * inv_root
    grad_scale = jnp.exp2(grad_expo.astype(jnp.float32))
    grad_code = jnp.clip(rotated / grad_scale[:, :, None], -4.0, 4.0).astype(jnp.bfloat16)
    scaled = grad_code.astype(jnp.float32) * grad_scale[:, :, None]
    decoded = jnp.einsum('rbi,ij->rbj', scaled, table, precision=lax.Precision.HIGHEST) * inv_root * sign[None]
    delta = lax.optimization_barrier(jnp.sum(decoded, axis=0)) / REPLICAS
    new_momentum = 0.9 * momentum + delta
    new_params = params - 0.7 * (delta + 0.9 * new_momentum)
    param_scale = jnp.exp2(param_expo.astype(jnp.float32))
    fragment_codes = jnp.clip(new_params / param_scale[:, None], -4.0, 4.0).astype(jnp.bfloat16)
    return (new_params, new_momentum, fragment_codes)
```

```python
import jax
import jax.numpy as jnp
import numpy as np
from jax import lax
from jax.experimental import pallas as pl
from jax.experimental.pallas import tpu as pltpu
from jax.sharding import Mesh
from jax.sharding import PartitionSpec as P

SIZES = (("zl", 4), ("c", 2), ("x", 4), ("zh", 2), ("y", 8))


def hadamard(width):
    index = np.arange(width)
    common = index[:, None] & index[None, :]
    parity = np.zeros((width, width), np.int32)
    for bit in range(width.bit_length() - 1):
        parity = parity + (common >> bit & 1)
    return (1 - 2 * (parity % 2)).astype(np.float32)


def exact_dot(values, table):
    total = None
    for _ in range(3):
        part = values.astype(jnp.bfloat16)
        values = values - part.astype(jnp.float32)
        product = jnp.dot(part, table, preferred_element_type=jnp.float32)
        total = product if total is None else total + product
    return total


def encode_kernel(grad_ref, expo_ref, bits_ref, table_ref, out_ref):
    width = grad_ref.shape[1]
    sign = (2 * bits_ref[...] - 1).astype(jnp.float32)
    rotated = exact_dot(grad_ref[...] * sign, table_ref[...]) * (width**-0.5)
    limit = 4.0 * jnp.exp2(expo_ref[...].astype(jnp.float32))
    out_ref[...] = jnp.clip(rotated, -limit, limit).astype(out_ref.dtype)


def update_kernel(terms_ref, bits_ref, params_ref, momentum_ref, expo_ref, table_ref,
                  new_params_ref, new_momentum_ref, codes_ref):
    replicas, _, width = terms_ref.shape
    total = terms_ref[0].astype(jnp.float32)
    for replica in range(1, replicas):
        total = total + terms_ref[replica].astype(jnp.float32)
    sign = (2 * bits_ref[...] - 1).astype(jnp.float32)
    delta = exact_dot(total, table_ref[...]) * sign * (width**-0.5 / replicas)
    new_momentum = 0.9 * momentum_ref[...] + delta
    new_params = params_ref[...] - 0.7 * (delta + 0.9 * new_momentum)
    new_momentum_ref[...] = new_momentum
    new_params_ref[...] = new_params
    inverse = jnp.exp2(-expo_ref[...].astype(jnp.float32))
    codes = jnp.clip(new_params * inverse, -4.0, 4.0).astype(codes_ref.dtype)
    codes_ref[...] = jnp.broadcast_to(codes[None], codes_ref.shape)


def shift(value, axis, by):
    size = lax.axis_size(axis)
    return lax.ppermute(value, axis, [(i, (i + by) % size) for i in range(size)])


def per_device(pseudo_grad, grad_expo, sign_bits, params, momentum, param_expo):
    shard, width = sign_bits.shape
    owned = params.shape[0]
    replicas = lax.axis_size(("zl", "c"))
    table = jnp.asarray(hadamard(width), jnp.bfloat16)
    vmem = pl.BlockSpec(memory_space=pltpu.VMEM)

    terms = pl.pallas_call(
        encode_kernel,
        out_shape=jax.ShapeDtypeStruct((shard, width), jnp.bfloat16),
        in_specs=[vmem] * 4,
        out_specs=vmem,
    )(pseudo_grad[0], grad_expo[0][:, None], sign_bits, table)
    terms = lax.all_to_all(terms, ("zl", "c"), split_axis=0, concat_axis=0, tiled=True)

    me = lax.axis_index(("zl", "c"))
    own_bits = lax.dynamic_slice_in_dim(sign_bits, me * owned, owned, 0)
    line = ("zh", "y", "zl")
    chips = lax.axis_size(line)
    new_params, new_momentum, spread = pl.pallas_call(
        update_kernel,
        out_shape=(
            jax.ShapeDtypeStruct((owned, width), jnp.float32),
            jax.ShapeDtypeStruct((owned, width), jnp.float32),
            jax.ShapeDtypeStruct((chips, owned, width), jnp.bfloat16),
        ),
        in_specs=[vmem] * 6,
        out_specs=(vmem,) * 3,
    )(terms.reshape(replicas, owned, width), own_bits, params, momentum, param_expo[:, None], table)

    plane = lax.all_to_all(spread, line, split_axis=0, concat_axis=0, tiled=True)
    planes = lax.axis_size("x")
    x, core = lax.axis_index("x"), lax.axis_index("c")
    whole = jnp.zeros((planes, chips, 2, owned, width), jnp.bfloat16)
    for by in (0, 1, -1, 2):
        mine = plane if by == 0 else shift(plane, "x", by)
        other = shift(mine, "c", 1)
        at = lax.rem(x - by + planes, planes)
        for side, piece in ((core, mine), (1 - core, other)):
            whole = lax.dynamic_update_slice(
                whole, piece[None, :, None], (at, 0, side, 0, 0)
            )
    return new_params, new_momentum, whole.reshape(-1, width)


def solution(mesh):
    names, sizes = zip(*SIZES)
    cut = Mesh(mesh.devices.reshape(sizes), names)
    outer, dev = ("zl", "c"), ("x", "zh", "y")
    owner = dev + outer
    in_specs = (P(outer, dev, None), P(outer, dev), P(dev, None),
                P(owner, None), P(owner, None), P(owner))
    out_specs = (P(owner, None), P(owner, None), P())
    return jax.shard_map(
        per_device, mesh=cut, in_specs=in_specs, out_specs=out_specs, check_vma=False
    )
```

```python
import jax
import jax.numpy as jnp
import numpy as np
from jax import lax
from jax.experimental import pallas as pl
from jax.experimental.pallas import tpu as pltpu
from jax.sharding import Mesh
from jax.sharding import PartitionSpec as P

SIZES = (("zl", 4), ("c", 2), ("x", 4), ("zh", 2), ("y", 8))
AXES = tuple(name for name, _ in SIZES)
BITS = (0, 1)


def device(x, y, z, core):
    x, y, z = x % 4, y % 8, z % 8
    return (((z % 4 * 2 + core) * 4 + x) * 2 + z // 4) * 8 + y


def classes():
    return [
        [
            device(2 * xh + px, 2 * yh + py, 4 * zh + 2 * zm + pz, core)
            for xh in BITS
            for zh in BITS
            for yh in range(4)
            for zm in BITS
        ]
        for px in BITS
        for py in BITS
        for pz in BITS
        for core in BITS
    ]


def cubes():
    return [
        [
            device(2 * xh + way * px, 2 * yh + way * py, 2 * zm + way * pz, core)
            for px in BITS
            for py in BITS
            for pz in BITS
        ]
        for core, way in ((0, 1), (1, -1))
        for xh in range(2)
        for yh in range(4)
        for zm in range(4)
    ]


def hadamard(width):
    index = np.arange(width)
    common = index[:, None] & index[None, :]
    parity = np.zeros((width, width), np.int32)
    for bit in range(width.bit_length() - 1):
        parity = parity + (common >> bit & 1)
    return (1 - 2 * (parity % 2)).astype(np.float32)


def exact_dot(values, table):
    total = None
    for _ in range(3):
        part = values.astype(jnp.bfloat16)
        values = values - part.astype(jnp.float32)
        product = jnp.dot(part, table, preferred_element_type=jnp.float32)
        total = product if total is None else total + product
    return total


def encode_kernel(grad_ref, expo_ref, bits_ref, table_ref, out_ref):
    width = grad_ref.shape[1]
    sign = (2 * bits_ref[...] - 1).astype(jnp.float32)
    rotated = exact_dot(grad_ref[...] * sign, table_ref[...]) * (width**-0.5)
    limit = 4.0 * jnp.exp2(expo_ref[...].astype(jnp.float32))
    out_ref[...] = jnp.clip(rotated, -limit, limit).astype(out_ref.dtype)


def update_kernel(terms_ref, bits_ref, params_ref, momentum_ref, expo_ref, table_ref,
                  new_params_ref, new_momentum_ref, codes_ref):
    replicas, _, width = terms_ref.shape
    total = terms_ref[0].astype(jnp.float32)
    for replica in range(1, replicas):
        total = total + terms_ref[replica].astype(jnp.float32)
    sign = (2 * bits_ref[...] - 1).astype(jnp.float32)
    delta = exact_dot(total, table_ref[...]) * sign * (width**-0.5 / replicas)
    new_momentum = 0.9 * momentum_ref[...] + delta
    new_params = params_ref[...] - 0.7 * (delta + 0.9 * new_momentum)
    new_momentum_ref[...] = new_momentum
    new_params_ref[...] = new_params
    inverse = jnp.exp2(-expo_ref[...].astype(jnp.float32))
    codes_ref[...] = jnp.clip(new_params * inverse, -4.0, 4.0).astype(codes_ref.dtype)


def place_kernel(side_ref, part_ref, *refs):
    out_ref, sems = refs[-2:]
    side = side_ref[0]
    copies = []
    for px in BITS:
        for py in BITS:
            for pz in BITS:
                for xh in BITS:
                    for zh in BITS:
                        copies.append(
                            pltpu.make_async_copy(
                                part_ref.at[px, py, pz, xh, zh],
                                out_ref.at[2 * xh + px, zh, :, py, :, pz, side],
                                sems.at[len(copies)],
                            )
                        )
    for copy in copies:
        copy.start()
    for copy in copies:
        copy.wait()


def place(side, part, whole=None):
    owned, width = part.shape[-2:]
    shape = jax.ShapeDtypeStruct((4, 2, 4, 2, 2, 2, 2, owned, width), part.dtype)
    given = (side, part) if whole is None else (side, part, whole)
    smem = pl.BlockSpec(memory_space=pltpu.SMEM)
    anywhere = pl.BlockSpec(memory_space=pl.ANY)
    return pl.pallas_call(
        place_kernel,
        out_shape=shape,
        in_specs=[smem] + [anywhere] * (len(given) - 1),
        out_specs=anywhere,
        scratch_shapes=[pltpu.SemaphoreType.DMA((32,))],
        input_output_aliases={} if whole is None else {2: 0},
        cost_estimate=pl.CostEstimate(
            flops=0, bytes_accessed=2 * part.size * 2, transcendentals=0
        ),
    )(*given)


def gather(value, groups):
    copies = jnp.broadcast_to(value[None], (len(groups[0]),) + value.shape)
    return lax.all_to_all(
        copies.reshape((-1,) + value.shape[1:]), AXES, split_axis=0, concat_axis=0,
        axis_index_groups=groups, tiled=True,
    )


def per_device(pseudo_grad, grad_expo, sign_bits, params, momentum, param_expo):
    shard, width = sign_bits.shape
    owned = params.shape[0]
    replicas = lax.axis_size(("zl", "c"))
    table = jnp.asarray(hadamard(width), jnp.bfloat16)
    vmem = pl.BlockSpec(memory_space=pltpu.VMEM)

    terms = pl.pallas_call(
        encode_kernel,
        out_shape=jax.ShapeDtypeStruct((shard, width), jnp.bfloat16),
        in_specs=[vmem] * 4,
        out_specs=vmem,
    )(pseudo_grad[0], grad_expo[0][:, None], sign_bits, table)
    terms = lax.all_to_all(terms, ("zl", "c"), split_axis=0, concat_axis=0, tiled=True)

    me = lax.axis_index(("zl", "c"))
    own_bits = lax.dynamic_slice_in_dim(sign_bits, me * owned, owned, 0)
    new_params, new_momentum, codes = pl.pallas_call(
        update_kernel,
        out_shape=(
            jax.ShapeDtypeStruct((owned, width), jnp.float32),
            jax.ShapeDtypeStruct((owned, width), jnp.float32),
            jax.ShapeDtypeStruct((owned, width), jnp.bfloat16),
        ),
        in_specs=[vmem] * 6,
        out_specs=(vmem,) * 3,
    )(terms.reshape(replicas, owned, width), own_bits, params, momentum, param_expo[:, None], table)

    mine = gather(gather(codes, classes()), cubes())
    other = lax.ppermute(mine, "c", [(0, 1), (1, 0)])
    parts = (2, 2, 2, 2, 2, 4, 2, owned, width)
    core = lax.axis_index("c").astype(jnp.int32)[None]
    whole = place(core, mine.reshape(parts))
    whole = place(1 - core, other.reshape(parts), whole)
    return new_params, new_momentum, whole.reshape(-1, width)


def solution(mesh):
    names, sizes = zip(*SIZES)
    cut = Mesh(mesh.devices.reshape(sizes), names)
    outer, dev = ("zl", "c"), ("x", "zh", "y")
    owner = dev + outer
    in_specs = (P(outer, dev, None), P(outer, dev), P(dev, None),
                P(owner, None), P(owner, None), P(owner))
    out_specs = (P(owner, None), P(owner, None), P())
    return jax.shard_map(
        per_device, mesh=cut, in_specs=in_specs, out_specs=out_specs, check_vma=False
    )
```

```python
import jax
import jax.numpy as jnp
import numpy as np
from jax import lax
from jax.experimental import pallas as pl
from jax.experimental.pallas import tpu as pltpu
from jax.sharding import Mesh
from jax.sharding import PartitionSpec as P

SIZES = (("zl", 4), ("c", 2), ("x", 4), ("zh", 2), ("y", 8))
AXES = tuple(name for name, _ in SIZES)
BITS = (0, 1)


def device(x, y, z, core):
    x, y, z = x % 4, y % 8, z % 8
    return (((z % 4 * 2 + core) * 4 + x) * 2 + z // 4) * 8 + y


def classes():
    return [
        [
            device(2 * xh + px, 2 * yh + py, 4 * zh + 2 * zm + pz, core)
            for xh in BITS
            for zh in BITS
            for yh in range(4)
            for zm in BITS
        ]
        for px in BITS
        for py in BITS
        for pz in BITS
        for core in BITS
    ]


def cubes():
    return [
        [
            device(2 * xh + way * px, 2 * yh + way * py, 2 * zm + way * pz, core)
            for px in BITS
            for py in BITS
            for pz in BITS
        ]
        for core, way in ((0, 1), (1, -1))
        for xh in range(2)
        for yh in range(4)
        for zm in range(4)
    ]


def hadamard(width):
    index = np.arange(width)
    common = index[:, None] & index[None, :]
    parity = np.zeros((width, width), np.int32)
    for bit in range(width.bit_length() - 1):
        parity = parity + (common >> bit & 1)
    return (1 - 2 * (parity % 2)).astype(np.float32)


def exact_dot(values, table):
    total = None
    for _ in range(3):
        part = values.astype(jnp.bfloat16)
        values = values - part.astype(jnp.float32)
        product = jnp.dot(part, table, preferred_element_type=jnp.float32)
        total = product if total is None else total + product
    return total


def encode_kernel(grad_ref, expo_ref, bits_ref, table_ref, out_ref):
    width = grad_ref.shape[1]
    sign = (2 * bits_ref[...] - 1).astype(jnp.float32)
    rotated = exact_dot(grad_ref[...] * sign, table_ref[...]) * (width**-0.5)
    limit = 4.0 * jnp.exp2(expo_ref[...].astype(jnp.float32))
    out_ref[...] = jnp.clip(rotated, -limit, limit).astype(out_ref.dtype)


def update_kernel(terms_ref, bits_ref, params_ref, momentum_ref, expo_ref, table_ref,
                  new_params_ref, new_momentum_ref, codes_ref):
    replicas, _, width = terms_ref.shape
    total = terms_ref[0].astype(jnp.float32)
    for replica in range(1, replicas):
        total = total + terms_ref[replica].astype(jnp.float32)
    sign = (2 * bits_ref[...] - 1).astype(jnp.float32)
    delta = exact_dot(total, table_ref[...]) * sign * (width**-0.5 / replicas)
    new_momentum = 0.9 * momentum_ref[...] + delta
    new_params = params_ref[...] - 0.7 * (delta + 0.9 * new_momentum)
    new_momentum_ref[...] = new_momentum
    new_params_ref[...] = new_params
    inverse = jnp.exp2(-expo_ref[...].astype(jnp.float32))
    codes_ref[...] = jnp.clip(new_params * inverse, -4.0, 4.0).astype(codes_ref.dtype)


def place_kernel(core_ref, mine_ref, other_ref, out_ref):
    x = pl.program_id(0)
    core = core_ref[0]
    for side, part_ref in ((core, mine_ref), (1 - core, other_ref)):
        for py in BITS:
            for pz in BITS:
                out_ref[0, :, :, py, :, pz, side] = part_ref[x % 2, py, pz, x // 2]


def place(core, mine, other):
    owned, width = mine.shape[-2:]
    block = (2, 4, 2, 2, 2, 2, owned, width)
    vmem = pl.BlockSpec(memory_space=pltpu.VMEM)
    return pl.pallas_call(
        place_kernel,
        out_shape=jax.ShapeDtypeStruct((4,) + block, mine.dtype),
        grid=(4,),
        in_specs=[pl.BlockSpec(memory_space=pltpu.SMEM), vmem, vmem],
        out_specs=pl.BlockSpec((1,) + block, lambda x: (x,) + (0,) * len(block)),
        cost_estimate=pl.CostEstimate(
            flops=0, bytes_accessed=8 * mine.size, transcendentals=0
        ),
        compiler_params=pltpu.CompilerParams(vmem_limit_bytes=16 * 2**20),
    )(core, mine, other)


def gather(value, groups):
    copies = jnp.broadcast_to(value[None], (len(groups[0]),) + value.shape)
    return lax.all_to_all(
        copies.reshape((-1,) + value.shape[1:]), AXES, split_axis=0, concat_axis=0,
        axis_index_groups=groups, tiled=True,
    )


def per_device(pseudo_grad, grad_expo, sign_bits, params, momentum, param_expo):
    shard, width = sign_bits.shape
    owned = params.shape[0]
    replicas = lax.axis_size(("zl", "c"))
    table = jnp.asarray(hadamard(width), jnp.bfloat16)
    vmem = pl.BlockSpec(memory_space=pltpu.VMEM)

    terms = pl.pallas_call(
        encode_kernel,
        out_shape=jax.ShapeDtypeStruct((shard, width), jnp.bfloat16),
        in_specs=[vmem] * 4,
        out_specs=vmem,
    )(pseudo_grad[0], grad_expo[0][:, None], sign_bits, table)
    terms = lax.all_to_all(terms, ("zl", "c"), split_axis=0, concat_axis=0, tiled=True)

    me = lax.axis_index(("zl", "c"))
    own_bits = lax.dynamic_slice_in_dim(sign_bits, me * owned, owned, 0)
    new_params, new_momentum, codes = pl.pallas_call(
        update_kernel,
        out_shape=(
            jax.ShapeDtypeStruct((owned, width), jnp.float32),
            jax.ShapeDtypeStruct((owned, width), jnp.float32),
            jax.ShapeDtypeStruct((owned, width), jnp.bfloat16),
        ),
        in_specs=[vmem] * 6,
        out_specs=(vmem,) * 3,
    )(terms.reshape(replicas, owned, width), own_bits, params, momentum, param_expo[:, None], table)

    mine = gather(gather(codes, classes()), cubes())
    other = lax.ppermute(mine, "c", [(0, 1), (1, 0)])
    parts = (2, 2, 2, 2, 2, 4, 2, owned, width)
    core = lax.axis_index("c").astype(jnp.int32)[None]
    whole = place(core, mine.reshape(parts), other.reshape(parts))
    return new_params, new_momentum, whole.reshape(-1, width)


def solution(mesh):
    names, sizes = zip(*SIZES)
    cut = Mesh(mesh.devices.reshape(sizes), names)
    outer, dev = ("zl", "c"), ("x", "zh", "y")
    owner = dev + outer
    in_specs = (P(outer, dev, None), P(outer, dev), P(dev, None),
                P(owner, None), P(owner, None), P(owner))
    out_specs = (P(owner, None), P(owner, None), P())
    return jax.shard_map(
        per_device, mesh=cut, in_specs=in_specs, out_specs=out_specs, check_vma=False
    )
```

```python
import jax
import jax.numpy as jnp
import numpy as np
from jax import lax
from jax.experimental import pallas as pl
from jax.experimental.pallas import tpu as pltpu
from jax.sharding import Mesh
from jax.sharding import PartitionSpec as P

SIZES = (("zl", 4), ("c", 2), ("x", 4), ("zh", 2), ("y", 8))
AXES = tuple(name for name, _ in SIZES)
BITS = (0, 1)


def device(x, y, z, core):
    x, y, z = x % 4, y % 8, z % 8
    return (((z % 4 * 2 + core) * 4 + x) * 2 + z // 4) * 8 + y


def classes():
    return [
        [
            device(2 * xh + px, 2 * yh + py, 4 * zh + 2 * zm + pz, core)
            for xh in BITS
            for zh in BITS
            for yh in range(4)
            for zm in BITS
        ]
        for px in BITS
        for py in BITS
        for pz in BITS
        for core in BITS
    ]


def cubes():
    return [
        [
            device(2 * xh + way * px, 2 * yh + way * py, 2 * zm + way * pz, core)
            for px in BITS
            for py in BITS
            for pz in BITS
        ]
        for core, way in ((0, 1), (1, -1))
        for xh in range(2)
        for yh in range(4)
        for zm in range(4)
    ]


def hadamard(width):
    index = np.arange(width)
    common = index[:, None] & index[None, :]
    parity = np.zeros((width, width), np.int32)
    for bit in range(width.bit_length() - 1):
        parity = parity + (common >> bit & 1)
    return (1 - 2 * (parity % 2)).astype(np.float32)


def exact_dot(values, table):
    total = None
    for _ in range(3):
        part = values.astype(jnp.bfloat16)
        values = values - part.astype(jnp.float32)
        product = jnp.dot(part, table, preferred_element_type=jnp.float32)
        total = product if total is None else total + product
    return total


def column(row):
    n = row.shape[1]
    down = lax.broadcasted_iota(jnp.int32, (n, n), 0)
    along = lax.broadcasted_iota(jnp.int32, (n, n), 1)
    spread = jnp.where(down == along, jnp.broadcast_to(row, (n, n)), 0.0)
    return jnp.sum(spread, axis=1, keepdims=True)


def encode_kernel(me_ref, grad_in, expo_in, bits_in, table_in, params_in, momentum_in,
                  terms_ref, table_ref, params_ref, decayed_ref, own_sign_ref,
                  grad_ref, expo_ref, bits_ref, momentum_ref, sems):
    inward = (
        (grad_in, grad_ref),
        (expo_in, expo_ref),
        (bits_in, bits_ref),
        (table_in, table_ref),
        (params_in, params_ref),
        (momentum_in, momentum_ref),
    )
    copies = [
        pltpu.make_async_copy(source, target, sems.at[i])
        for i, (source, target) in enumerate(inward)
    ]
    for copy in copies:
        copy.start()
    for copy in copies:
        copy.wait()
    width = grad_ref.shape[1]
    owned = own_sign_ref.shape[0]
    replicas = grad_ref.shape[0] // owned
    sign = (2 * bits_ref[...] - 1).astype(jnp.float32)
    table = table_ref[...].astype(jnp.bfloat16)
    rotated = exact_dot(grad_ref[...] * sign, table) * (width**-0.5)
    limit = column(4.0 * jnp.exp2(expo_ref[...].astype(jnp.float32)))
    terms_ref[...] = jnp.clip(rotated, -limit, limit).astype(terms_ref.dtype)
    own = pl.ds(pl.multiple_of(me_ref[0] * owned, owned), owned)
    own_sign = (2 * bits_ref[own, :] - 1).astype(jnp.float32)
    own_sign_ref[...] = own_sign * (width**-0.5 / replicas)
    decayed_ref[...] = 0.9 * momentum_ref[...]


def encode(me, grad, expo, bits, table, params, momentum):
    shard, width = grad.shape
    owned = params.shape[0]
    f32 = jnp.float32
    smem = pl.BlockSpec(memory_space=pltpu.SMEM)
    vmem = pl.BlockSpec(memory_space=pltpu.VMEM)
    hbm = pl.BlockSpec(memory_space=pltpu.HBM)
    return pl.pallas_call(
        encode_kernel,
        out_shape=(
            jax.ShapeDtypeStruct((shard, width), jnp.bfloat16),
            jax.ShapeDtypeStruct((width, width), f32),
            jax.ShapeDtypeStruct((owned, width), f32),
            jax.ShapeDtypeStruct((owned, width), f32),
            jax.ShapeDtypeStruct((owned, width), f32),
        ),
        in_specs=[smem] + [hbm] * 6,
        out_specs=(vmem,) * 5,
        scratch_shapes=[
            pltpu.VMEM((shard, width), f32),
            pltpu.VMEM((1, shard), jnp.int32),
            pltpu.VMEM((shard, width), jnp.int32),
            pltpu.VMEM((owned, width), f32),
            pltpu.SemaphoreType.DMA((6,)),
        ],
        compiler_params=pltpu.CompilerParams(vmem_limit_bytes=4 * 2**20),
    )(
        me,
        *(
            pltpu.with_memory_space_constraint(value, pltpu.HBM)
            for value in (grad, expo, bits, table, params, momentum)
        ),
    )


def place_kernel(core_ref, mine_ref, other_ref, out_ref):
    x = pl.program_id(0)
    core = core_ref[0]
    for side, part_ref in ((core, mine_ref), (1 - core, other_ref)):
        for py in BITS:
            for pz in BITS:
                out_ref[0, :, :, py, :, pz, side] = part_ref[x % 2, py, pz, x // 2]


def place(core, mine, other):
    owned, width = mine.shape[-2:]
    block = (2, 4, 2, 2, 2, 2, owned, width)
    vmem = pl.BlockSpec(memory_space=pltpu.VMEM)
    return pl.pallas_call(
        place_kernel,
        out_shape=jax.ShapeDtypeStruct((4,) + block, mine.dtype),
        grid=(4,),
        in_specs=[pl.BlockSpec(memory_space=pltpu.SMEM), vmem, vmem],
        out_specs=pl.BlockSpec((1,) + block, lambda x: (x,) + (0,) * len(block)),
        cost_estimate=pl.CostEstimate(
            flops=0, bytes_accessed=8 * mine.size, transcendentals=0
        ),
        compiler_params=pltpu.CompilerParams(vmem_limit_bytes=16 * 2**20),
    )(core, mine, other)


def gather(value, groups):
    copies = jnp.broadcast_to(value[None], (len(groups[0]),) + value.shape)
    return lax.all_to_all(
        copies.reshape((-1,) + value.shape[1:]), AXES, split_axis=0, concat_axis=0,
        axis_index_groups=groups, tiled=True,
    )


def per_device(pseudo_grad, grad_expo, sign_bits, params, momentum, param_expo):
    owned, width = params.shape
    replicas = lax.axis_size(("zl", "c"))
    me = lax.axis_index(("zl", "c")).astype(jnp.int32)[None]
    table = jnp.asarray(hadamard(width))
    terms, table, params, decayed, own_sign = encode(
        me, pseudo_grad[0], grad_expo, sign_bits, table, params, momentum
    )
    terms = lax.all_to_all(terms, ("zl", "c"), split_axis=0, concat_axis=0, tiled=True)

    total = jnp.sum(terms.reshape(replicas, owned, width).astype(jnp.float32), axis=0)
    delta = jnp.dot(total, table, precision=lax.Precision.HIGHEST) * own_sign
    new_params = params - 0.7 * (delta + 0.9 * (decayed + delta))
    inverse = jnp.exp2(-param_expo.astype(jnp.float32))[:, None]
    codes = jnp.clip(new_params * inverse, -4.0, 4.0).astype(jnp.bfloat16)
    codes, delta = lax.optimization_barrier((codes, delta))
    new_momentum = decayed + delta
    new_params = params - 0.7 * (delta + 0.9 * new_momentum)

    mine = gather(gather(codes, classes()), cubes())
    other = lax.ppermute(mine, "c", [(0, 1), (1, 0)])
    parts = (2, 2, 2, 2, 2, 4, 2, owned, width)
    core = lax.axis_index("c").astype(jnp.int32)[None]
    whole = place(core, mine.reshape(parts), other.reshape(parts))
    return new_params, new_momentum, whole.reshape(-1, width)


def solution(mesh):
    names, sizes = zip(*SIZES)
    cut = Mesh(mesh.devices.reshape(sizes), names)
    outer, dev = ("zl", "c"), ("x", "zh", "y")
    owner = dev + outer
    in_specs = (P(outer, dev, None), P(outer, dev), P(dev, None),
                P(owner, None), P(owner, None), P(owner))
    out_specs = (P(owner, None), P(owner, None), P())
    return jax.shard_map(
        per_device, mesh=cut, in_specs=in_specs, out_specs=out_specs, check_vma=False
    )
```

```python
import jax
import jax.numpy as jnp
import numpy as np
from jax import lax
from jax.experimental import pallas as pl
from jax.experimental.pallas import tpu as pltpu
from jax.sharding import Mesh
from jax.sharding import PartitionSpec as P

SIZES = (("zl", 4), ("c", 2), ("x", 4), ("zh", 2), ("y", 8))
AXES = tuple(name for name, _ in SIZES)
CLASSES = 4


def device(x, y, z, core):
    x, y, z = x % 4, y % 8, z % 8
    return (((z % 4 * 2 + core) * 4 + x) * 2 + z // 4) * 8 + y


def chips():
    return [(x, y, z) for x in range(4) for y in range(8) for z in range(8)]


def classes():
    return [
        [
            device(kind - 2 * y - 3 * z, y, z, core)
            for zh in range(2)
            for y in range(8)
            for z in range(4 * zh, 4 * zh + 4)
        ]
        for kind in range(CLASSES)
        for core in (0, 1)
    ]


NEIGHBOURS = {
    1: ((1, 0, 0), (0, 0, -1)),
    2: ((0, 1, 0), (0, -1, 0)),
    3: ((-1, 0, 0), (0, 0, 1)),
}


def from_neighbours(step):
    return [
        (device(x + dx, y + dy, z + dz, core), device(x, y, z, core))
        for core, (dx, dy, dz) in enumerate(NEIGHBOURS[step])
        for x, y, z in chips()
    ]


def hadamard(width):
    index = np.arange(width)
    common = index[:, None] & index[None, :]
    parity = np.zeros((width, width), np.int32)
    for bit in range(width.bit_length() - 1):
        parity = parity + (common >> bit & 1)
    return (1 - 2 * (parity % 2)).astype(np.float32)


def exact_dot(values, table):
    total = None
    for _ in range(3):
        part = values.astype(jnp.bfloat16)
        values = values - part.astype(jnp.float32)
        product = jnp.dot(part, table, preferred_element_type=jnp.float32)
        total = product if total is None else total + product
    return total


def column(row):
    n = row.shape[1]
    down = lax.broadcasted_iota(jnp.int32, (n, n), 0)
    along = lax.broadcasted_iota(jnp.int32, (n, n), 1)
    spread = jnp.where(down == along, jnp.broadcast_to(row, (n, n)), 0.0)
    return jnp.sum(spread, axis=1, keepdims=True)


def encode_kernel(me_ref, grad_in, expo_in, bits_in, table_in, params_in, momentum_in,
                  terms_ref, table_ref, params_ref, decayed_ref, own_sign_ref,
                  grad_ref, expo_ref, bits_ref, momentum_ref, sems):
    inward = (
        (grad_in, grad_ref),
        (expo_in, expo_ref),
        (bits_in, bits_ref),
        (table_in, table_ref),
        (params_in, params_ref),
        (momentum_in, momentum_ref),
    )
    copies = [
        pltpu.make_async_copy(source, target, sems.at[i])
        for i, (source, target) in enumerate(inward)
    ]
    for copy in copies:
        copy.start()
    for copy in copies:
        copy.wait()
    width = grad_ref.shape[1]
    owned = own_sign_ref.shape[0]
    replicas = grad_ref.shape[0] // owned
    sign = (2 * bits_ref[...] - 1).astype(jnp.float32)
    table = table_ref[...].astype(jnp.bfloat16)
    rotated = exact_dot(grad_ref[...] * sign, table) * (width**-0.5)
    limit = column(4.0 * jnp.exp2(expo_ref[...].astype(jnp.float32)))
    terms_ref[...] = jnp.clip(rotated, -limit, limit).astype(terms_ref.dtype)
    own = pl.ds(pl.multiple_of(me_ref[0] * owned, owned), owned)
    own_sign = (2 * bits_ref[own, :] - 1).astype(jnp.float32)
    own_sign_ref[...] = own_sign * (width**-0.5 / replicas)
    decayed_ref[...] = 0.9 * momentum_ref[...]


def encode(me, grad, expo, bits, table, params, momentum):
    shard, width = grad.shape
    owned = params.shape[0]
    f32 = jnp.float32
    smem = pl.BlockSpec(memory_space=pltpu.SMEM)
    vmem = pl.BlockSpec(memory_space=pltpu.VMEM)
    hbm = pl.BlockSpec(memory_space=pltpu.HBM)
    return pl.pallas_call(
        encode_kernel,
        out_shape=(
            jax.ShapeDtypeStruct((shard, width), jnp.bfloat16),
            jax.ShapeDtypeStruct((width, width), f32),
            jax.ShapeDtypeStruct((owned, width), f32),
            jax.ShapeDtypeStruct((owned, width), f32),
            jax.ShapeDtypeStruct((owned, width), f32),
        ),
        in_specs=[smem] + [hbm] * 6,
        out_specs=(vmem,) * 5,
        scratch_shapes=[
            pltpu.VMEM((shard, width), f32),
            pltpu.VMEM((1, shard), jnp.int32),
            pltpu.VMEM((shard, width), jnp.int32),
            pltpu.VMEM((owned, width), f32),
            pltpu.SemaphoreType.DMA((6,)),
        ],
        compiler_params=pltpu.CompilerParams(vmem_limit_bytes=4 * 2**20),
    )(
        me,
        *(
            pltpu.with_memory_space_constraint(value, pltpu.HBM)
            for value in (grad, expo, bits, table, params, momentum)
        ),
    )


def place_kernel(spot_ref, *refs):
    out_ref = refs[-1]
    kind, core = spot_ref[0], spot_ref[1]
    for step in range(CLASSES):
        for side, part_ref in ((core, refs[step]), (1 - core, refs[CLASSES + step])):
            for y in range(out_ref.shape[2]):
                for z in range(out_ref.shape[3]):
                    x = lax.rem(kind + step + 2 * y + z, 4)
                    out_ref[x, 0, y, z, side] = part_ref[pl.program_id(0), y, z]


def place(kind, core, mine, others):
    width = mine[0].shape[-1]
    parts = [part.reshape(4, 4, 4, -1, width) for part in (*mine, *others)]
    owned = parts[0].shape[3]
    block = (4, 1, 4, 4, 2, owned, width)
    vmem = pl.BlockSpec(memory_space=pltpu.VMEM)
    return pl.pallas_call(
        place_kernel,
        out_shape=jax.ShapeDtypeStruct((4, 4, 4, 4, 2, owned, width), parts[0].dtype),
        grid=(4,),
        in_specs=[pl.BlockSpec(memory_space=pltpu.SMEM)] + [vmem] * len(parts),
        out_specs=pl.BlockSpec(block, lambda i: (0, i, 0, 0, 0, 0, 0)),
        cost_estimate=pl.CostEstimate(
            flops=0, bytes_accessed=32 * parts[0].size, transcendentals=0
        ),
        compiler_params=pltpu.CompilerParams(vmem_limit_bytes=16 * 2**20),
    )(jnp.stack([kind, core]), *parts)


def gather(value, groups):
    copies = jnp.broadcast_to(value[None], (len(groups[0]),) + value.shape)
    return lax.all_to_all(
        copies.reshape((-1,) + value.shape[1:]), AXES, split_axis=0, concat_axis=0,
        axis_index_groups=groups, tiled=True,
    )


def per_device(pseudo_grad, grad_expo, sign_bits, params, momentum, param_expo):
    owned, width = params.shape
    replicas = lax.axis_size(("zl", "c"))
    me = lax.axis_index(("zl", "c")).astype(jnp.int32)[None]
    table = jnp.asarray(hadamard(width))
    terms, table, params, decayed, own_sign = encode(
        me, pseudo_grad[0], grad_expo, sign_bits, table, params, momentum
    )
    terms = lax.all_to_all(terms, ("zl", "c"), split_axis=0, concat_axis=0, tiled=True)

    total = jnp.sum(terms.reshape(replicas, owned, width).astype(jnp.float32), axis=0)
    delta = jnp.dot(total, table, precision=lax.Precision.HIGHEST) * own_sign
    new_params = params - 0.7 * (delta + 0.9 * (decayed + delta))
    inverse = jnp.exp2(-param_expo.astype(jnp.float32))[:, None]
    codes = jnp.clip(new_params * inverse, -4.0, 4.0).astype(jnp.bfloat16)
    codes, delta = lax.optimization_barrier((codes, delta))
    new_momentum = decayed + delta
    new_params = params - 0.7 * (delta + 0.9 * new_momentum)

    own = gather(codes, classes())
    mine = [own] + [
        lax.ppermute(own, AXES, from_neighbours(step)) for step in range(1, CLASSES)
    ]
    others = [lax.ppermute(part, "c", [(0, 1), (1, 0)]) for part in mine]
    x, y, zl, core = (lax.axis_index(name) for name in ("x", "y", "zl", "c"))
    whole = place(lax.rem(x + 2 * y + 3 * zl, CLASSES), core, mine, others)
    return new_params, new_momentum, whole.reshape(-1, width)


def solution(mesh):
    names, sizes = zip(*SIZES)
    cut = Mesh(mesh.devices.reshape(sizes), names)
    outer, dev = ("zl", "c"), ("x", "zh", "y")
    owner = dev + outer
    in_specs = (P(outer, dev, None), P(outer, dev), P(dev, None),
                P(owner, None), P(owner, None), P(owner))
    out_specs = (P(owner, None), P(owner, None), P())
    return jax.shard_map(
        per_device, mesh=cut, in_specs=in_specs, out_specs=out_specs, check_vma=False
    )
```

```python
import jax
import jax.numpy as jnp
import numpy as np
from jax import lax
from jax.experimental import pallas as pl
from jax.experimental.pallas import tpu as pltpu
from jax.sharding import Mesh
from jax.sharding import PartitionSpec as P

SIZES = (("zl", 4), ("c", 2), ("x", 4), ("zh", 2), ("y", 8))
AXES = tuple(name for name, _ in SIZES)
BITS = (0, 1)


def device(x, y, z, core):
    x, y, z = x % 4, y % 8, z % 8
    return (((z % 4 * 2 + core) * 4 + x) * 2 + z // 4) * 8 + y


def classes():
    return [
        [
            device(row + 2 * z, 2 * yh + (side + z) % 2, z, core)
            for z in range(8)
            for yh in range(4)
        ]
        for row in range(4)
        for side in BITS
        for core in BITS
    ]


def cubes():
    def place_of(chip):
        x, y, z = chip
        row = (x + 2 * z) % 4
        return row % 2, row // 2, (y + z) % 2

    groups = []
    for core in BITS:
        for x in range(core, 4, 2):
            for y in range(core, 8, 2):
                for z in range(core, 8, 2):
                    cube = [
                        ((x + i) % 4, (y + j) % 8, (z + k) % 8)
                        for i in BITS
                        for j in BITS
                        for k in BITS
                    ]
                    cube.sort(key=place_of)
                    groups.append([device(*chip, core) for chip in cube])
    return groups


def hadamard(width):
    index = np.arange(width)
    common = index[:, None] & index[None, :]
    parity = np.zeros((width, width), np.int32)
    for bit in range(width.bit_length() - 1):
        parity = parity + (common >> bit & 1)
    return (1 - 2 * (parity % 2)).astype(np.float32)


def exact_dot(values, table):
    total = None
    for _ in range(3):
        part = values.astype(jnp.bfloat16)
        values = values - part.astype(jnp.float32)
        product = jnp.dot(part, table, preferred_element_type=jnp.float32)
        total = product if total is None else total + product
    return total


def column(row):
    n = row.shape[1]
    down = lax.broadcasted_iota(jnp.int32, (n, n), 0)
    along = lax.broadcasted_iota(jnp.int32, (n, n), 1)
    spread = jnp.where(down == along, jnp.broadcast_to(row, (n, n)), 0.0)
    return jnp.sum(spread, axis=1, keepdims=True)


def encode_kernel(me_ref, grad_in, expo_in, bits_in, table_in, params_in, momentum_in,
                  param_expo_in, terms_ref, table_ref, params_ref, decayed_ref,
                  own_sign_ref, inverse_ref, grad_ref, expo_ref, bits_ref, momentum_ref,
                  param_expo_ref, sems):
    inward = (
        (grad_in, grad_ref),
        (expo_in, expo_ref),
        (bits_in, bits_ref),
        (table_in, table_ref),
        (params_in, params_ref),
        (momentum_in, momentum_ref),
        (param_expo_in, param_expo_ref),
    )
    copies = [
        pltpu.make_async_copy(source, target, sems.at[i])
        for i, (source, target) in enumerate(inward)
    ]
    for copy in copies:
        copy.start()
    for copy in copies:
        copy.wait()
    width = grad_ref.shape[1]
    owned = own_sign_ref.shape[0]
    replicas = grad_ref.shape[0] // owned
    sign = (2 * bits_ref[...] - 1).astype(jnp.float32)
    table = table_ref[...].astype(jnp.bfloat16)
    rotated = exact_dot(grad_ref[...] * sign, table) * (width**-0.5)
    limit = column(4.0 * jnp.exp2(expo_ref[...].astype(jnp.float32)))
    terms_ref[...] = jnp.clip(rotated, -limit, limit).astype(terms_ref.dtype)
    own = pl.ds(pl.multiple_of(me_ref[0] * owned, owned), owned)
    own_sign = (2 * bits_ref[own, :] - 1).astype(jnp.float32)
    own_sign_ref[...] = own_sign * (width**-0.5 / replicas)
    decayed_ref[...] = 0.9 * momentum_ref[...]
    inverse = column(jnp.exp2(-param_expo_ref[...].astype(jnp.float32)))
    inverse_ref[...] = jnp.broadcast_to(inverse, inverse_ref.shape)


def encode(me, grad, expo, bits, table, params, momentum, param_expo):
    shard, width = grad.shape
    owned = params.shape[0]
    f32 = jnp.float32
    smem = pl.BlockSpec(memory_space=pltpu.SMEM)
    vmem = pl.BlockSpec(memory_space=pltpu.VMEM)
    hbm = pl.BlockSpec(memory_space=pltpu.HBM)
    return pl.pallas_call(
        encode_kernel,
        out_shape=(
            jax.ShapeDtypeStruct((shard, width), jnp.bfloat16),
            jax.ShapeDtypeStruct((width, width), f32),
            jax.ShapeDtypeStruct((owned, width), f32),
            jax.ShapeDtypeStruct((owned, width), f32),
            jax.ShapeDtypeStruct((owned, width), f32),
            jax.ShapeDtypeStruct((owned, width), f32),
        ),
        in_specs=[smem] + [hbm] * 7,
        out_specs=(vmem,) * 6,
        scratch_shapes=[
            pltpu.VMEM((shard, width), f32),
            pltpu.VMEM((1, shard), jnp.int32),
            pltpu.VMEM((shard, width), jnp.int32),
            pltpu.VMEM((owned, width), f32),
            pltpu.VMEM((1, owned), jnp.int32),
            pltpu.SemaphoreType.DMA((7,)),
        ],
        compiler_params=pltpu.CompilerParams(vmem_limit_bytes=4 * 2**20),
    )(
        me,
        *(
            pltpu.with_memory_space_constraint(value, pltpu.HBM)
            for value in (grad, expo, bits, table, params, momentum, param_expo)
        ),
    )


def fill(core_ref, mine_ref, other_ref, out_ref):
    xh = pl.program_id(0)
    core = core_ref[0]
    for side, part_ref in ((core, mine_ref), (1 - core, other_ref)):
        for zl in range(4):
            half = xh if zl % 2 == 0 else 1 - xh
            for py in BITS:
                for zh in BITS:
                    out_ref[0, 0, zh, :, py, zl, side] = part_ref[
                        half, (py + zl) % 2, 4 * zh + zl
                    ]


def place_even_kernel(core_ref, mine_ref, other_ref, params_ref, decayed_ref, delta_ref,
                      out_ref, new_params_ref, new_momentum_ref):
    fill(core_ref, mine_ref, other_ref, out_ref)
    delta = delta_ref[...]
    new_momentum = decayed_ref[...] + delta
    new_momentum_ref[...] = new_momentum
    new_params_ref[...] = params_ref[...] - 0.7 * (delta + 0.9 * new_momentum)


def place_odd_kernel(core_ref, mine_ref, other_ref, even_ref, out_ref):
    fill(core_ref, mine_ref, other_ref, out_ref)


def place(core, mine, other, owner=None, even=None):
    owned, width = mine.shape[-2:]
    px = 0 if even is None else 1
    block = (2, 4, 2, 4, 2, owned, width)
    smem = pl.BlockSpec(memory_space=pltpu.SMEM)
    vmem = pl.BlockSpec(memory_space=pltpu.VMEM)
    whole = jax.ShapeDtypeStruct((2, 2) + block, mine.dtype)
    whole_spec = pl.BlockSpec((1, 1) + block, lambda xh: (xh, px) + (0,) * len(block))
    small = jax.ShapeDtypeStruct((owned, width), jnp.float32)
    small_spec = pl.BlockSpec((owned, width), lambda xh: (0, 0))
    common = dict(
        grid=(2,),
        cost_estimate=pl.CostEstimate(
            flops=0, bytes_accessed=8 * mine.size, transcendentals=0
        ),
        compiler_params=pltpu.CompilerParams(vmem_limit_bytes=16 * 2**20),
    )
    if even is None:
        return pl.pallas_call(
            place_even_kernel,
            out_shape=(whole, small, small),
            in_specs=[smem] + [vmem] * 5,
            out_specs=(whole_spec, small_spec, small_spec),
            **common,
        )(core, mine, other, *owner)
    return pl.pallas_call(
        place_odd_kernel,
        out_shape=whole,
        in_specs=[smem, vmem, vmem, pl.BlockSpec(memory_space=pl.ANY)],
        out_specs=whole_spec,
        input_output_aliases={3: 0},
        **common,
    )(core, mine, other, even)


def gather(value, groups):
    copies = jnp.broadcast_to(value[None], (len(groups[0]),) + value.shape)
    return lax.all_to_all(
        copies.reshape((-1,) + value.shape[1:]), AXES, split_axis=0, concat_axis=0,
        axis_index_groups=groups, tiled=True,
    )


def per_device(pseudo_grad, grad_expo, sign_bits, params, momentum, param_expo):
    owned, width = params.shape
    replicas = lax.axis_size(("zl", "c"))
    me = lax.axis_index(("zl", "c")).astype(jnp.int32)[None]
    table = jnp.asarray(hadamard(width))
    terms, table, params, decayed, own_sign, inverse = encode(
        me, pseudo_grad[0], grad_expo, sign_bits, table, params, momentum, param_expo[None]
    )
    terms = lax.all_to_all(terms, ("zl", "c"), split_axis=0, concat_axis=0, tiled=True)

    total = jnp.sum(terms.reshape(replicas, owned, width).astype(jnp.float32), axis=0)
    delta = jnp.dot(total, table, precision=lax.Precision.HIGHEST) * own_sign
    new_params = params - 0.7 * (delta + 0.9 * (decayed + delta))
    codes = jnp.clip(new_params * inverse, -4.0, 4.0).astype(jnp.bfloat16)
    mine = gather(gather(codes, classes()), cubes())
    halves = [
        half.reshape(2, 2, 8, 4, owned, width) for half in jnp.split(mine, 2)
    ]
    others = [lax.ppermute(half, "c", [(0, 1), (1, 0)]) for half in halves]
    core = lax.axis_index("c").astype(jnp.int32)[None]
    whole, new_params, new_momentum = place(
        core, halves[0], others[0], owner=(params, decayed, delta)
    )
    whole = place(core, halves[1], others[1], even=whole)
    return new_params, new_momentum, whole.reshape(-1, width)


def solution(mesh):
    names, sizes = zip(*SIZES)
    cut = Mesh(mesh.devices.reshape(sizes), names)
    outer, dev = ("zl", "c"), ("x", "zh", "y")
    owner = dev + outer
    in_specs = (P(outer, dev, None), P(outer, dev), P(dev, None),
                P(owner, None), P(owner, None), P(owner))
    out_specs = (P(owner, None), P(owner, None), P())
    return jax.shard_map(
        per_device, mesh=cut, in_specs=in_specs, out_specs=out_specs, check_vma=False
    )
```

```python
import jax
import jax.numpy as jnp
import numpy as np
from jax import lax
from jax.experimental import pallas as pl
from jax.experimental.pallas import tpu as pltpu
from jax.sharding import Mesh
from jax.sharding import PartitionSpec as P

SIZES = (("zl", 4), ("c", 2), ("x", 4), ("zh", 2), ("y", 8))
AXES = tuple(name for name, _ in SIZES)
BITS = (0, 1)


def device(x, y, z, core):
    x, y, z = x % 4, y % 8, z % 8
    return (((z % 4 * 2 + core) * 4 + x) * 2 + z // 4) * 8 + y


def classes():
    return [
        [
            device(row + 2 * z, 2 * yh + (side + z) % 2, z, core)
            for z in range(8)
            for yh in range(4)
        ]
        for row in range(4)
        for side in BITS
        for core in BITS
    ]


def cubes():
    def place_of(chip):
        x, y, z = chip
        row = (x + 2 * z) % 4
        return row % 2, row // 2, (y + z) % 2

    groups = []
    for core, start in enumerate(((0, 0, 1), (1, 1, 0))):
        for x in range(start[0], 4, 2):
            for y in range(start[1], 8, 2):
                for z in range(start[2], 8, 2):
                    cube = [
                        ((x + i) % 4, (y + j) % 8, (z + k) % 8)
                        for i in BITS
                        for j in BITS
                        for k in BITS
                    ]
                    cube.sort(key=place_of)
                    groups.append([device(*chip, core) for chip in cube])
    return groups


def hadamard(width):
    index = np.arange(width)
    common = index[:, None] & index[None, :]
    parity = np.zeros((width, width), np.int32)
    for bit in range(width.bit_length() - 1):
        parity = parity + (common >> bit & 1)
    return (1 - 2 * (parity % 2)).astype(np.float32)


def exact_dot(values, table):
    total = None
    for _ in range(3):
        part = values.astype(jnp.bfloat16)
        values = values - part.astype(jnp.float32)
        product = jnp.dot(part, table, preferred_element_type=jnp.float32)
        total = product if total is None else total + product
    return total


def column(row):
    n = row.shape[1]
    down = lax.broadcasted_iota(jnp.int32, (n, n), 0)
    along = lax.broadcasted_iota(jnp.int32, (n, n), 1)
    spread = jnp.where(down == along, jnp.broadcast_to(row, (n, n)), 0.0)
    return jnp.sum(spread, axis=1, keepdims=True)


def encode_kernel(me_ref, grad_in, expo_in, bits_in, table_in, params_in, momentum_in,
                  param_expo_in, terms_ref, table_ref, params_ref, decayed_ref,
                  own_sign_ref, inverse_ref, grad_ref, expo_ref, bits_ref, momentum_ref,
                  param_expo_ref, sems):
    inward = (
        (grad_in, grad_ref),
        (expo_in, expo_ref),
        (bits_in, bits_ref),
        (table_in, table_ref),
        (params_in, params_ref),
        (momentum_in, momentum_ref),
        (param_expo_in, param_expo_ref),
    )
    copies = [
        pltpu.make_async_copy(source, target, sems.at[i])
        for i, (source, target) in enumerate(inward)
    ]
    for copy in copies:
        copy.start()
    for copy in copies:
        copy.wait()
    width = grad_ref.shape[1]
    owned = own_sign_ref.shape[0]
    replicas = grad_ref.shape[0] // owned
    sign = (2 * bits_ref[...] - 1).astype(jnp.float32)
    table = table_ref[...].astype(jnp.bfloat16)
    rotated = exact_dot(grad_ref[...] * sign, table) * (width**-0.5)
    limit = column(4.0 * jnp.exp2(expo_ref[...].astype(jnp.float32)))
    terms_ref[...] = jnp.clip(rotated, -limit, limit).astype(terms_ref.dtype)
    own = pl.ds(pl.multiple_of(me_ref[0] * owned, owned), owned)
    own_sign = (2 * bits_ref[own, :] - 1).astype(jnp.float32)
    own_sign_ref[...] = own_sign * (width**-0.5 / replicas)
    decayed_ref[...] = 0.9 * momentum_ref[...]
    inverse = column(jnp.exp2(-param_expo_ref[...].astype(jnp.float32)))
    inverse_ref[...] = jnp.broadcast_to(inverse, inverse_ref.shape)


def encode(me, grad, expo, bits, table, params, momentum, param_expo):
    shard, width = grad.shape
    owned = params.shape[0]
    f32 = jnp.float32
    smem = pl.BlockSpec(memory_space=pltpu.SMEM)
    vmem = pl.BlockSpec(memory_space=pltpu.VMEM)
    hbm = pl.BlockSpec(memory_space=pltpu.HBM)
    return pl.pallas_call(
        encode_kernel,
        out_shape=(
            jax.ShapeDtypeStruct((shard, width), jnp.bfloat16),
            jax.ShapeDtypeStruct((width, width), f32),
            jax.ShapeDtypeStruct((owned, width), f32),
            jax.ShapeDtypeStruct((owned, width), f32),
            jax.ShapeDtypeStruct((owned, width), f32),
            jax.ShapeDtypeStruct((owned, width), f32),
        ),
        in_specs=[smem] + [hbm] * 7,
        out_specs=(vmem,) * 6,
        scratch_shapes=[
            pltpu.VMEM((shard, width), f32),
            pltpu.VMEM((1, shard), jnp.int32),
            pltpu.VMEM((shard, width), jnp.int32),
            pltpu.VMEM((owned, width), f32),
            pltpu.VMEM((1, owned), jnp.int32),
            pltpu.SemaphoreType.DMA((7,)),
        ],
        compiler_params=pltpu.CompilerParams(vmem_limit_bytes=4 * 2**20),
    )(
        me,
        *(
            pltpu.with_memory_space_constraint(value, pltpu.HBM)
            for value in (grad, expo, bits, table, params, momentum, param_expo)
        ),
    )


def fill(core_ref, mine_ref, other_ref, out_ref):
    xh = pl.program_id(0)
    core = core_ref[0]
    for side, part_ref in ((core, mine_ref), (1 - core, other_ref)):
        for zl in range(4):
            half = xh if zl % 2 == 0 else 1 - xh
            for py in BITS:
                for zh in BITS:
                    out_ref[0, 0, zh, :, py, zl, side] = part_ref[
                        half, (py + zl) % 2, 4 * zh + zl
                    ]


def place_even_kernel(core_ref, mine_ref, other_ref, params_ref, decayed_ref, delta_ref,
                      out_ref, new_params_ref, new_momentum_ref):
    fill(core_ref, mine_ref, other_ref, out_ref)
    delta = delta_ref[...]
    new_momentum = decayed_ref[...] + delta
    new_momentum_ref[...] = new_momentum
    new_params_ref[...] = params_ref[...] - 0.7 * (delta + 0.9 * new_momentum)


def place_odd_kernel(core_ref, mine_ref, other_ref, even_ref, out_ref):
    fill(core_ref, mine_ref, other_ref, out_ref)


def place(core, mine, other, owner=None, even=None):
    owned, width = mine.shape[-2:]
    px = 0 if even is None else 1
    block = (2, 4, 2, 4, 2, owned, width)
    smem = pl.BlockSpec(memory_space=pltpu.SMEM)
    vmem = pl.BlockSpec(memory_space=pltpu.VMEM)
    whole = jax.ShapeDtypeStruct((2, 2) + block, mine.dtype)
    whole_spec = pl.BlockSpec((1, 1) + block, lambda xh: (xh, px) + (0,) * len(block))
    small = jax.ShapeDtypeStruct((owned, width), jnp.float32)
    small_spec = pl.BlockSpec((owned, width), lambda xh: (0, 0))
    common = dict(
        grid=(2,),
        cost_estimate=pl.CostEstimate(
            flops=0, bytes_accessed=8 * mine.size, transcendentals=0
        ),
        compiler_params=pltpu.CompilerParams(vmem_limit_bytes=16 * 2**20),
    )
    if even is None:
        return pl.pallas_call(
            place_even_kernel,
            out_shape=(whole, small, small),
            in_specs=[smem] + [vmem] * 5,
            out_specs=(whole_spec, small_spec, small_spec),
            **common,
        )(core, mine, other, *owner)
    return pl.pallas_call(
        place_odd_kernel,
        out_shape=whole,
        in_specs=[smem, vmem, vmem, pl.BlockSpec(memory_space=pl.ANY)],
        out_specs=whole_spec,
        input_output_aliases={3: 0},
        **common,
    )(core, mine, other, even)


def gather(value, groups):
    copies = jnp.broadcast_to(value[None], (len(groups[0]),) + value.shape)
    return lax.all_to_all(
        copies.reshape((-1,) + value.shape[1:]), AXES, split_axis=0, concat_axis=0,
        axis_index_groups=groups, tiled=True,
    )


def per_device(pseudo_grad, grad_expo, sign_bits, params, momentum, param_expo):
    owned, width = params.shape
    replicas = lax.axis_size(("zl", "c"))
    me = lax.axis_index(("zl", "c")).astype(jnp.int32)[None]
    table = jnp.asarray(hadamard(width))
    terms, table, params, decayed, own_sign, inverse = encode(
        me, pseudo_grad[0], grad_expo, sign_bits, table, params, momentum, param_expo[None]
    )
    terms = lax.all_to_all(terms, ("zl", "c"), split_axis=0, concat_axis=0, tiled=True)

    total = jnp.sum(terms.reshape(replicas, owned, width).astype(jnp.float32), axis=0)
    delta = jnp.dot(total, table, precision=lax.Precision.HIGHEST) * own_sign
    new_params = params - 0.7 * (delta + 0.9 * (decayed + delta))
    codes = jnp.clip(new_params * inverse, -4.0, 4.0).astype(jnp.bfloat16)
    mine = gather(gather(codes, classes()), cubes())
    halves = [
        half.reshape(2, 2, 8, 4, owned, width) for half in jnp.split(mine, 2)
    ]
    others = [lax.ppermute(half, "c", [(0, 1), (1, 0)]) for half in halves]
    core = lax.axis_index("c").astype(jnp.int32)[None]
    whole, new_params, new_momentum = place(
        core, halves[0], others[0], owner=(params, decayed, delta)
    )
    whole = place(core, halves[1], others[1], even=whole)
    return new_params, new_momentum, whole.reshape(-1, width)


def solution(mesh):
    names, sizes = zip(*SIZES)
    cut = Mesh(mesh.devices.reshape(sizes), names)
    outer, dev = ("zl", "c"), ("x", "zh", "y")
    owner = dev + outer
    in_specs = (P(outer, dev, None), P(outer, dev), P(dev, None),
                P(owner, None), P(owner, None), P(owner))
    out_specs = (P(owner, None), P(owner, None), P())
    return jax.shard_map(
        per_device, mesh=cut, in_specs=in_specs, out_specs=out_specs, check_vma=False
    )
```

```python
import jax
import jax.numpy as jnp
import numpy as np
from jax import lax
from jax.experimental import pallas as pl
from jax.experimental.pallas import tpu as pltpu
from jax.sharding import Mesh
from jax.sharding import PartitionSpec as P

SIZES = (("zl", 4), ("c", 2), ("x", 4), ("zh", 2), ("y", 8))
AXES = tuple(name for name, _ in SIZES)
BITS = (0, 1)
EARLY = 5


def device(x, y, z, core):
    x, y, z = x % 4, y % 8, z % 8
    return (((z % 4 * 2 + core) * 4 + x) * 2 + z // 4) * 8 + y


def classes():
    return [
        [
            device(row + 2 * z, 2 * yh + (side + z) % 2, z, core)
            for z in range(8)
            for yh in range(4)
        ]
        for row in range(4)
        for side in BITS
        for core in BITS
    ]


def cubes():
    def place_of(chip):
        x, y, z = chip
        row = (x + 2 * z) % 4
        return row % 2, row // 2, (y + z) % 2

    groups = []
    for core, start in enumerate(((0, 0, 1), (1, 1, 0))):
        for x in range(start[0], 4, 2):
            for y in range(start[1], 8, 2):
                for z in range(start[2], 8, 2):
                    cube = [
                        ((x + i) % 4, (y + j) % 8, (z + k) % 8)
                        for i in BITS
                        for j in BITS
                        for k in BITS
                    ]
                    cube.sort(key=place_of)
                    groups.append([device(*chip, core) for chip in cube])
    return groups


def hadamard(width):
    index = np.arange(width)
    common = index[:, None] & index[None, :]
    parity = np.zeros((width, width), np.int32)
    for bit in range(width.bit_length() - 1):
        parity = parity + (common >> bit & 1)
    return (1 - 2 * (parity % 2)).astype(np.float32)


def exact_dot(values, table):
    total = None
    for _ in range(3):
        part = values.astype(jnp.bfloat16)
        values = values - part.astype(jnp.float32)
        product = jnp.dot(part, table, preferred_element_type=jnp.float32)
        total = product if total is None else total + product
    return total


def column(row):
    n = row.shape[1]
    down = lax.broadcasted_iota(jnp.int32, (n, n), 0)
    along = lax.broadcasted_iota(jnp.int32, (n, n), 1)
    spread = jnp.where(down == along, jnp.broadcast_to(row, (n, n)), 0.0)
    return jnp.sum(spread, axis=1, keepdims=True)


def encode_kernel(me_ref, grad_in, expo_in, bits_in, table_in, params_in, momentum_in,
                  param_expo_in, terms_ref, table_ref, params_ref, decayed_ref,
                  own_sign_ref, inverse_ref, grad_ref, expo_ref, bits_ref, momentum_ref,
                  param_expo_ref, sems):
    inward = (
        (grad_in, grad_ref),
        (expo_in, expo_ref),
        (bits_in, bits_ref),
        (table_in, table_ref),
        (params_in, params_ref),
        (momentum_in, momentum_ref),
        (param_expo_in, param_expo_ref),
    )
    copies = [
        pltpu.make_async_copy(source, target, sems.at[i])
        for i, (source, target) in enumerate(inward)
    ]
    for copy in copies:
        copy.start()
    for copy in copies:
        copy.wait()
    width = grad_ref.shape[1]
    owned = own_sign_ref.shape[0]
    replicas = grad_ref.shape[0] // owned
    sign = (2 * bits_ref[...] - 1).astype(jnp.float32)
    table = table_ref[...].astype(jnp.bfloat16)
    rotated = exact_dot(grad_ref[...] * sign, table) * (width**-0.5)
    limit = column(4.0 * jnp.exp2(expo_ref[...].astype(jnp.float32)))
    terms_ref[...] = jnp.clip(rotated, -limit, limit).astype(terms_ref.dtype)
    own = pl.ds(pl.multiple_of(me_ref[0] * owned, owned), owned)
    own_sign = (2 * bits_ref[own, :] - 1).astype(jnp.float32)
    own_sign_ref[...] = own_sign * (width**-0.5 / replicas)
    decayed_ref[...] = 0.9 * momentum_ref[...]
    inverse = column(jnp.exp2(-param_expo_ref[...].astype(jnp.float32)))
    inverse_ref[...] = jnp.broadcast_to(inverse, inverse_ref.shape)


def encode(me, grad, expo, bits, table, params, momentum, param_expo):
    shard, width = grad.shape
    owned = params.shape[0]
    f32 = jnp.float32
    smem = pl.BlockSpec(memory_space=pltpu.SMEM)
    vmem = pl.BlockSpec(memory_space=pltpu.VMEM)
    hbm = pl.BlockSpec(memory_space=pltpu.HBM)
    return pl.pallas_call(
        encode_kernel,
        out_shape=(
            jax.ShapeDtypeStruct((shard, width), jnp.bfloat16),
            jax.ShapeDtypeStruct((width, width), f32),
            jax.ShapeDtypeStruct((owned, width), f32),
            jax.ShapeDtypeStruct((owned, width), f32),
            jax.ShapeDtypeStruct((owned, width), f32),
            jax.ShapeDtypeStruct((owned, width), f32),
        ),
        in_specs=[smem] + [hbm] * 7,
        out_specs=(vmem,) * 6,
        scratch_shapes=[
            pltpu.VMEM((shard, width), f32),
            pltpu.VMEM((1, shard), jnp.int32),
            pltpu.VMEM((shard, width), jnp.int32),
            pltpu.VMEM((owned, width), f32),
            pltpu.VMEM((1, owned), jnp.int32),
            pltpu.SemaphoreType.DMA((7,)),
        ],
        compiler_params=pltpu.CompilerParams(vmem_limit_bytes=4 * 2**20),
    )(
        me,
        *(
            pltpu.with_memory_space_constraint(value, pltpu.HBM)
            for value in (grad, expo, bits, table, params, momentum, param_expo)
        ),
    )


def fill(core_ref, mine, other, out_ref):
    core = core_ref[0]
    for xh in BITS:

        @pl.when(pl.program_id(0) == xh)
        def _():
            for side, part in ((core, mine), (1 - core, other)):
                for zl in range(4):
                    for py in BITS:
                        for zh in BITS:
                            out_ref[0, 0, zh, :, py, zl, side] = part(
                                (xh + zl) % 2, (py + zl) % 2
                            )[4 * zh + zl]


def place_even_kernel(core_ref, mine_ref, other_ref, params_ref, decayed_ref, delta_ref,
                      out_ref, new_params_ref, new_momentum_ref):
    fill(
        core_ref,
        lambda half, side: mine_ref.at[2 * half + side],
        lambda half, side: other_ref.at[2 * half + side],
        out_ref,
    )
    delta = delta_ref[...]
    new_momentum = decayed_ref[...] + delta
    new_momentum_ref[...] = new_momentum
    new_params_ref[...] = params_ref[...] - 0.7 * (delta + 0.9 * new_momentum)


def place_odd_kernel(core_ref, mine_ref, early_ref, late_ref, even_ref, out_ref):
    early = early_ref.shape[0]

    def other(half, side):
        at = 4 + 2 * half + side
        return early_ref.at[at] if at < early else late_ref.at[at - early]

    fill(core_ref, lambda half, side: mine_ref.at[4 + 2 * half + side], other, out_ref)


def place(core, mine, early, owner=None, late=None, even=None):
    owned, width = mine.shape[-2:]
    px = 0 if even is None else 1
    block = (2, 4, 2, 4, 2, owned, width)
    smem = pl.BlockSpec(memory_space=pltpu.SMEM)
    vmem = pl.BlockSpec(memory_space=pltpu.VMEM)
    whole = jax.ShapeDtypeStruct((2, 2) + block, mine.dtype)
    whole_spec = pl.BlockSpec((1, 1) + block, lambda xh: (xh, px) + (0,) * len(block))
    small = jax.ShapeDtypeStruct((owned, width), jnp.float32)
    small_spec = pl.BlockSpec((owned, width), lambda xh: (0, 0))
    common = dict(
        grid=(2,),
        cost_estimate=pl.CostEstimate(
            flops=0, bytes_accessed=4 * mine.size, transcendentals=0
        ),
        compiler_params=pltpu.CompilerParams(vmem_limit_bytes=16 * 2**20),
    )
    if even is None:
        return pl.pallas_call(
            place_even_kernel,
            out_shape=(whole, small, small),
            in_specs=[smem] + [vmem] * 5,
            out_specs=(whole_spec, small_spec, small_spec),
            **common,
        )(core, mine, early, *owner)
    return pl.pallas_call(
        place_odd_kernel,
        out_shape=whole,
        in_specs=[smem, vmem, vmem, vmem, pl.BlockSpec(memory_space=pl.ANY)],
        out_specs=whole_spec,
        input_output_aliases={4: 0},
        **common,
    )(core, mine, early, late, even)


def gather(value, groups):
    copies = jnp.broadcast_to(value[None], (len(groups[0]),) + value.shape)
    return lax.all_to_all(
        copies.reshape((-1,) + value.shape[1:]), AXES, split_axis=0, concat_axis=0,
        axis_index_groups=groups, tiled=True,
    )


def per_device(pseudo_grad, grad_expo, sign_bits, params, momentum, param_expo):
    owned, width = params.shape
    replicas = lax.axis_size(("zl", "c"))
    me = lax.axis_index(("zl", "c")).astype(jnp.int32)[None]
    table = jnp.asarray(hadamard(width))
    terms, table, params, decayed, own_sign, inverse = encode(
        me, pseudo_grad[0], grad_expo, sign_bits, table, params, momentum, param_expo[None]
    )
    terms = lax.all_to_all(terms, ("zl", "c"), split_axis=0, concat_axis=0, tiled=True)

    total = jnp.sum(terms.reshape(replicas, owned, width).astype(jnp.float32), axis=0)
    delta = jnp.dot(total, table, precision=lax.Precision.HIGHEST) * own_sign
    new_params = params - 0.7 * (delta + 0.9 * (decayed + delta))
    codes = jnp.clip(new_params * inverse, -4.0, 4.0).astype(jnp.bfloat16)
    mine = gather(gather(codes, classes()), cubes())
    mine = mine.reshape(8, 8, 4, owned, width)
    early, late = (
        lax.ppermute(part, "c", [(0, 1), (1, 0)]) for part in (mine[:EARLY], mine[EARLY:])
    )
    core = lax.axis_index("c").astype(jnp.int32)[None]
    whole, new_params, new_momentum = place(
        core, mine, early, owner=(params, decayed, delta)
    )
    whole = place(core, mine, early, late=late, even=whole)
    return new_params, new_momentum, whole.reshape(-1, width)


def solution(mesh):
    names, sizes = zip(*SIZES)
    cut = Mesh(mesh.devices.reshape(sizes), names)
    outer, dev = ("zl", "c"), ("x", "zh", "y")
    owner = dev + outer
    in_specs = (P(outer, dev, None), P(outer, dev), P(dev, None),
                P(owner, None), P(owner, None), P(owner))
    out_specs = (P(owner, None), P(owner, None), P())
    return jax.shard_map(
        per_device, mesh=cut, in_specs=in_specs, out_specs=out_specs, check_vma=False
    )
```

```python
import jax
import jax.numpy as jnp
import numpy as np
from jax import lax
from jax.experimental import pallas as pl
from jax.experimental.pallas import tpu as pltpu
from jax.sharding import Mesh
from jax.sharding import PartitionSpec as P

SIZES = (("zl", 4), ("c", 2), ("x", 4), ("zh", 2), ("y", 8))
AXES = tuple(name for name, _ in SIZES)
BITS = (0, 1)
EARLY = 5


def device(x, y, z, core):
    x, y, z = x % 4, y % 8, z % 8
    return (((z % 4 * 2 + core) * 4 + x) * 2 + z // 4) * 8 + y


def classes():
    return [
        [
            device(row + 2 * z, 2 * yh + (side + z) % 2, z, core)
            for z in range(8)
            for yh in range(4)
        ]
        for row in range(4)
        for side in BITS
        for core in BITS
    ]


def cubes():
    def place_of(chip):
        x, y, z = chip
        row = (x + 2 * z) % 4
        return row % 2, row // 2, (y + z) % 2

    groups = []
    for core, start in enumerate(((0, 0, 1), (1, 1, 0))):
        for x in range(start[0], 4, 2):
            for y in range(start[1], 8, 2):
                for z in range(start[2], 8, 2):
                    cube = [
                        ((x + i) % 4, (y + j) % 8, (z + k) % 8)
                        for i in BITS
                        for j in BITS
                        for k in BITS
                    ]
                    cube.sort(key=place_of)
                    groups.append([device(*chip, core) for chip in cube])
    return groups


def hadamard(width):
    index = np.arange(width)
    common = index[:, None] & index[None, :]
    parity = np.zeros((width, width), np.int32)
    for bit in range(width.bit_length() - 1):
        parity = parity + (common >> bit & 1)
    return (1 - 2 * (parity % 2)).astype(np.float32)


def dot_parts(values, table):
    high = values.astype(jnp.bfloat16)
    low = (values - high.astype(jnp.float32)).astype(jnp.bfloat16)
    parts = jnp.concatenate([high, low])
    both = jnp.dot(parts, table, preferred_element_type=jnp.float32)
    return both[: values.shape[0]] + both[values.shape[0] :]


def column(row):
    n = row.shape[1]
    down = lax.broadcasted_iota(jnp.int32, (n, n), 0)
    along = lax.broadcasted_iota(jnp.int32, (n, n), 1)
    spread = jnp.where(down == along, jnp.broadcast_to(row, (n, n)), 0.0)
    return jnp.sum(spread, axis=1, keepdims=True)


def encode_kernel(me_ref, grad_in, expo_in, bits_in, table_in, params_in, momentum_in,
                  param_expo_in, terms_ref, table_ref, params_ref, decayed_ref,
                  own_sign_ref, inverse_ref, grad_ref, expo_ref, bits_ref, momentum_ref,
                  param_expo_ref, sems):
    inward = (
        (grad_in, grad_ref),
        (expo_in, expo_ref),
        (bits_in, bits_ref),
        (table_in, table_ref),
        (params_in, params_ref),
        (momentum_in, momentum_ref),
        (param_expo_in, param_expo_ref),
    )
    copies = [
        pltpu.make_async_copy(source, target, sems.at[i])
        for i, (source, target) in enumerate(inward)
    ]
    for copy in copies:
        copy.start()
    for copy in copies:
        copy.wait()
    width = grad_ref.shape[1]
    owned = own_sign_ref.shape[0]
    replicas = grad_ref.shape[0] // owned
    sign = (2 * bits_ref[...] - 1).astype(jnp.float32)
    rotated = dot_parts(grad_ref[...] * sign, table_ref[...]) * (width**-0.5)
    limit = column(4.0 * jnp.exp2(expo_ref[...].astype(jnp.float32)))
    terms_ref[...] = jnp.clip(rotated, -limit, limit).astype(terms_ref.dtype)
    own = pl.ds(pl.multiple_of(me_ref[0] * owned, owned), owned)
    own_sign = (2 * bits_ref[own, :] - 1).astype(jnp.float32)
    own_sign_ref[...] = own_sign * (width**-0.5 / replicas)
    decayed_ref[...] = 0.9 * momentum_ref[...]
    inverse = column(jnp.exp2(-param_expo_ref[...].astype(jnp.float32)))
    inverse_ref[...] = jnp.broadcast_to(inverse, inverse_ref.shape)


def encode(me, grad, expo, bits, table, params, momentum, param_expo):
    shard, width = grad.shape
    owned = params.shape[0]
    f32 = jnp.float32
    smem = pl.BlockSpec(memory_space=pltpu.SMEM)
    vmem = pl.BlockSpec(memory_space=pltpu.VMEM)
    hbm = pl.BlockSpec(memory_space=pltpu.HBM)
    return pl.pallas_call(
        encode_kernel,
        out_shape=(
            jax.ShapeDtypeStruct((shard, width), jnp.bfloat16),
            jax.ShapeDtypeStruct((width, width), jnp.bfloat16),
            jax.ShapeDtypeStruct((owned, width), f32),
            jax.ShapeDtypeStruct((owned, width), f32),
            jax.ShapeDtypeStruct((owned, width), f32),
            jax.ShapeDtypeStruct((owned, width), f32),
        ),
        in_specs=[smem] + [hbm] * 7,
        out_specs=(vmem,) * 6,
        scratch_shapes=[
            pltpu.VMEM((shard, width), f32),
            pltpu.VMEM((1, shard), jnp.int32),
            pltpu.VMEM((shard, width), jnp.int32),
            pltpu.VMEM((owned, width), f32),
            pltpu.VMEM((1, owned), jnp.int32),
            pltpu.SemaphoreType.DMA((7,)),
        ],
        compiler_params=pltpu.CompilerParams(vmem_limit_bytes=4 * 2**20),
    )(
        me,
        *(
            pltpu.with_memory_space_constraint(value, pltpu.HBM)
            for value in (grad, expo, bits, table, params, momentum, param_expo)
        ),
    )


def fill(core_ref, mine, other, out_ref):
    core = core_ref[0]
    for xh in BITS:

        @pl.when(pl.program_id(0) == xh)
        def _():
            for side, part in ((core, mine), (1 - core, other)):
                for zl in range(4):
                    for py in BITS:
                        for zh in BITS:
                            out_ref[0, 0, zh, :, py, zl, side] = part(
                                (xh + zl) % 2, (py + zl) % 2
                            )[4 * zh + zl]


def place_even_kernel(core_ref, mine_ref, other_ref, params_ref, decayed_ref, delta_ref,
                      out_ref, new_params_ref, new_momentum_ref):
    fill(
        core_ref,
        lambda half, side: mine_ref.at[2 * half + side],
        lambda half, side: other_ref.at[2 * half + side],
        out_ref,
    )
    delta = delta_ref[...]
    new_momentum = decayed_ref[...] + delta
    new_momentum_ref[...] = new_momentum
    new_params_ref[...] = params_ref[...] - 0.7 * (delta + 0.9 * new_momentum)


def place_odd_kernel(core_ref, mine_ref, early_ref, late_ref, even_ref, out_ref):
    early = early_ref.shape[0]

    def other(half, side):
        at = 4 + 2 * half + side
        return early_ref.at[at] if at < early else late_ref.at[at - early]

    fill(core_ref, lambda half, side: mine_ref.at[4 + 2 * half + side], other, out_ref)


def place(core, mine, early, owner=None, late=None, even=None):
    owned, width = mine.shape[-2:]
    px = 0 if even is None else 1
    block = (2, 4, 2, 4, 2, owned, width)
    smem = pl.BlockSpec(memory_space=pltpu.SMEM)
    vmem = pl.BlockSpec(memory_space=pltpu.VMEM)
    whole = jax.ShapeDtypeStruct((2, 2) + block, mine.dtype)
    whole_spec = pl.BlockSpec((1, 1) + block, lambda xh: (xh, px) + (0,) * len(block))
    small = jax.ShapeDtypeStruct((owned, width), jnp.float32)
    small_spec = pl.BlockSpec((owned, width), lambda xh: (0, 0))
    common = dict(
        grid=(2,),
        cost_estimate=pl.CostEstimate(
            flops=0, bytes_accessed=4 * mine.size, transcendentals=0
        ),
        compiler_params=pltpu.CompilerParams(vmem_limit_bytes=16 * 2**20),
    )
    if even is None:
        return pl.pallas_call(
            place_even_kernel,
            out_shape=(whole, small, small),
            in_specs=[smem] + [vmem] * 5,
            out_specs=(whole_spec, small_spec, small_spec),
            **common,
        )(core, mine, early, *owner)
    return pl.pallas_call(
        place_odd_kernel,
        out_shape=whole,
        in_specs=[smem, vmem, vmem, vmem, pl.BlockSpec(memory_space=pl.ANY)],
        out_specs=whole_spec,
        input_output_aliases={4: 0},
        **common,
    )(core, mine, early, late, even)


def gather(value, groups):
    copies = jnp.broadcast_to(value[None], (len(groups[0]),) + value.shape)
    return lax.all_to_all(
        copies.reshape((-1,) + value.shape[1:]), AXES, split_axis=0, concat_axis=0,
        axis_index_groups=groups, tiled=True,
    )


def per_device(pseudo_grad, grad_expo, sign_bits, params, momentum, param_expo):
    owned, width = params.shape
    replicas = lax.axis_size(("zl", "c"))
    me = lax.axis_index(("zl", "c")).astype(jnp.int32)[None]
    table = jnp.asarray(hadamard(width), jnp.bfloat16)
    terms, table, params, decayed, own_sign, inverse = encode(
        me, pseudo_grad[0], grad_expo, sign_bits, table, params, momentum, param_expo[None]
    )
    terms = lax.all_to_all(terms, ("zl", "c"), split_axis=0, concat_axis=0, tiled=True)

    total = jnp.sum(terms.reshape(replicas, owned, width).astype(jnp.float32), axis=0)
    high = lax.reduce_precision(total, 8, 7)
    delta = sum(
        jnp.dot(part.astype(jnp.bfloat16), table, preferred_element_type=jnp.float32)
        for part in (high, total - high)
    )
    delta = delta * own_sign
    new_params = params - 0.7 * (delta + 0.9 * (decayed + delta))
    codes = jnp.clip(new_params * inverse, -4.0, 4.0).astype(jnp.bfloat16)
    mine = gather(gather(codes, classes()), cubes())
    mine = mine.reshape(8, 8, 4, owned, width)
    early, late = (
        lax.ppermute(part, "c", [(0, 1), (1, 0)]) for part in (mine[:EARLY], mine[EARLY:])
    )
    core = lax.axis_index("c").astype(jnp.int32)[None]
    whole, new_params, new_momentum = place(
        core, mine, early, owner=(params, decayed, delta)
    )
    whole = place(core, mine, early, late=late, even=whole)
    return new_params, new_momentum, whole.reshape(-1, width)


def solution(mesh):
    names, sizes = zip(*SIZES)
    cut = Mesh(mesh.devices.reshape(sizes), names)
    outer, dev = ("zl", "c"), ("x", "zh", "y")
    owner = dev + outer
    in_specs = (P(outer, dev, None), P(outer, dev), P(dev, None),
                P(owner, None), P(owner, None), P(owner))
    out_specs = (P(owner, None), P(owner, None), P())
    return jax.shard_map(
        per_device, mesh=cut, in_specs=in_specs, out_specs=out_specs, check_vma=False
    )
```

```python
import jax
import jax.numpy as jnp
import numpy as np
from jax import lax
from jax.experimental import pallas as pl
from jax.experimental.pallas import tpu as pltpu
from jax.sharding import Mesh
from jax.sharding import PartitionSpec as P

SIZES = (("zl", 4), ("c", 2), ("x", 4), ("zh", 2), ("y", 8))
AXES = tuple(name for name, _ in SIZES)
BITS = (0, 1)
EARLY = 5


def device(x, y, z, core):
    x, y, z = x % 4, y % 8, z % 8
    return (((z % 4 * 2 + core) * 4 + x) * 2 + z // 4) * 8 + y


def classes():
    return [
        [
            device(row + 2 * z, 2 * yh + (side + z) % 2, z, core)
            for z in range(8)
            for yh in range(4)
        ]
        for row in range(4)
        for side in BITS
        for core in BITS
    ]


def cubes():
    def place_of(chip):
        x, y, z = chip
        row = (x + 2 * z) % 4
        return row % 2, row // 2, (y + z) % 2

    groups = []
    for core, start in enumerate(((0, 0, 1), (1, 1, 0))):
        for x in range(start[0], 4, 2):
            for y in range(start[1], 8, 2):
                for z in range(start[2], 8, 2):
                    cube = [
                        ((x + i) % 4, (y + j) % 8, (z + k) % 8)
                        for i in BITS
                        for j in BITS
                        for k in BITS
                    ]
                    cube.sort(key=place_of)
                    groups.append([device(*chip, core) for chip in cube])
    return groups


def hadamard(width):
    index = np.arange(width)
    common = index[:, None] & index[None, :]
    parity = np.zeros((width, width), np.int32)
    for bit in range(width.bit_length() - 1):
        parity = parity + (common >> bit & 1)
    return (1 - 2 * (parity % 2)).astype(np.float32)


def exact_dot(values, table):
    total = None
    for _ in range(3):
        part = values.astype(jnp.bfloat16)
        values = values - part.astype(jnp.float32)
        product = jnp.dot(part, table, preferred_element_type=jnp.float32)
        total = product if total is None else total + product
    return total


def column(row):
    n = row.shape[1]
    down = lax.broadcasted_iota(jnp.int32, (n, n), 0)
    along = lax.broadcasted_iota(jnp.int32, (n, n), 1)
    spread = jnp.where(down == along, jnp.broadcast_to(row, (n, n)), 0.0)
    return jnp.sum(spread, axis=1, keepdims=True)


def encode_kernel(me_ref, grad_in, expo_in, bits_in, table_in, params_in, momentum_in,
                  param_expo_in, terms_ref, table_ref, params_ref, decayed_ref,
                  own_sign_ref, inverse_ref, grad_ref, expo_ref, bits_ref, momentum_ref,
                  param_expo_ref, sems):
    inward = (
        (grad_in, grad_ref),
        (expo_in, expo_ref),
        (bits_in, bits_ref),
        (table_in, table_ref),
        (params_in, params_ref),
        (momentum_in, momentum_ref),
        (param_expo_in, param_expo_ref),
    )
    copies = [
        pltpu.make_async_copy(source, target, sems.at[i])
        for i, (source, target) in enumerate(inward)
    ]
    for copy in copies:
        copy.start()
    for copy in copies:
        copy.wait()
    width = grad_ref.shape[1]
    owned = own_sign_ref.shape[0]
    replicas = grad_ref.shape[0] // owned
    sign = (2 * bits_ref[...] - 1).astype(jnp.float32)
    table = table_ref[...].astype(jnp.bfloat16)
    rotated = exact_dot(grad_ref[...] * sign, table) * (width**-0.5)
    limit = column(4.0 * jnp.exp2(expo_ref[...].astype(jnp.float32)))
    terms_ref[...] = jnp.clip(rotated, -limit, limit).astype(terms_ref.dtype)
    own = pl.ds(pl.multiple_of(me_ref[0] * owned, owned), owned)
    own_sign = (2 * bits_ref[own, :] - 1).astype(jnp.float32)
    own_sign_ref[...] = own_sign * (width**-0.5 / replicas)
    decayed_ref[...] = 0.9 * momentum_ref[...]
    inverse = column(jnp.exp2(-param_expo_ref[...].astype(jnp.float32)))
    inverse_ref[...] = jnp.broadcast_to(inverse, inverse_ref.shape)


def encode(me, grad, expo, bits, table, params, momentum, param_expo):
    shard, width = grad.shape
    owned = params.shape[0]
    f32 = jnp.float32
    smem = pl.BlockSpec(memory_space=pltpu.SMEM)
    vmem = pl.BlockSpec(memory_space=pltpu.VMEM)
    hbm = pl.BlockSpec(memory_space=pltpu.HBM)
    return pl.pallas_call(
        encode_kernel,
        out_shape=(
            jax.ShapeDtypeStruct((shard, width), jnp.bfloat16),
            jax.ShapeDtypeStruct((width, width), f32),
            jax.ShapeDtypeStruct((owned, width), f32),
            jax.ShapeDtypeStruct((owned, width), f32),
            jax.ShapeDtypeStruct((owned, width), f32),
            jax.ShapeDtypeStruct((owned, width), f32),
        ),
        in_specs=[smem] + [hbm] * 7,
        out_specs=(vmem,) * 6,
        scratch_shapes=[
            pltpu.VMEM((shard, width), f32),
            pltpu.VMEM((1, shard), jnp.int32),
            pltpu.VMEM((shard, width), jnp.int32),
            pltpu.VMEM((owned, width), f32),
            pltpu.VMEM((1, owned), jnp.int32),
            pltpu.SemaphoreType.DMA((7,)),
        ],
        compiler_params=pltpu.CompilerParams(vmem_limit_bytes=4 * 2**20),
    )(
        me,
        *(
            pltpu.with_memory_space_constraint(value, pltpu.HBM)
            for value in (grad, expo, bits, table, params, momentum, param_expo)
        ),
    )


def fill(core_ref, mine, other, out_ref):
    core = core_ref[0]
    zh = pl.program_id(1)
    for xh in BITS:

        @pl.when(pl.program_id(0) == xh)
        def _():
            for side, part in ((core, mine), (1 - core, other)):
                for zl in range(4):
                    for py in BITS:
                        out_ref[0, 0, 0, :, py, zl, side] = part(
                            (xh + zl) % 2, (py + zl) % 2
                        )[4 * zh + zl]


def place_even_kernel(core_ref, mine_ref, other_ref, params_ref, decayed_ref, delta_ref,
                      out_ref, new_params_ref, new_momentum_ref):
    fill(
        core_ref,
        lambda half, side: mine_ref.at[2 * half + side],
        lambda half, side: other_ref.at[2 * half + side],
        out_ref,
    )
    delta = delta_ref[...]
    new_momentum = decayed_ref[...] + delta
    new_momentum_ref[...] = new_momentum
    new_params_ref[...] = params_ref[...] - 0.7 * (delta + 0.9 * new_momentum)


def place_odd_kernel(core_ref, mine_ref, early_ref, late_ref, even_ref, out_ref):
    early = early_ref.shape[0]

    def other(half, side):
        at = 4 + 2 * half + side
        return early_ref.at[at] if at < early else late_ref.at[at - early]

    fill(core_ref, lambda half, side: mine_ref.at[4 + 2 * half + side], other, out_ref)


def place(core, mine, early, owner=None, late=None, even=None):
    owned, width = mine.shape[-2:]
    px = 0 if even is None else 1
    block = (4, 2, 4, 2, owned, width)
    smem = pl.BlockSpec(memory_space=pltpu.SMEM)
    vmem = pl.BlockSpec(memory_space=pltpu.VMEM)
    whole = jax.ShapeDtypeStruct((2, 2, 2) + block, mine.dtype)
    whole_spec = pl.BlockSpec(
        (1, 1, 1) + block, lambda xh, zh: (xh, px, zh) + (0,) * len(block)
    )
    small = jax.ShapeDtypeStruct((owned, width), jnp.float32)
    small_spec = pl.BlockSpec((owned, width), lambda xh, zh: (0, 0))
    common = dict(
        grid=(2, 2),
        cost_estimate=pl.CostEstimate(
            flops=0, bytes_accessed=4 * mine.size, transcendentals=0
        ),
        compiler_params=pltpu.CompilerParams(vmem_limit_bytes=16 * 2**20),
    )
    if even is None:
        return pl.pallas_call(
            place_even_kernel,
            out_shape=(whole, small, small),
            in_specs=[smem] + [vmem] * 5,
            out_specs=(whole_spec, small_spec, small_spec),
            **common,
        )(core, mine, early, *owner)
    return pl.pallas_call(
        place_odd_kernel,
        out_shape=whole,
        in_specs=[smem, vmem, vmem, vmem, pl.BlockSpec(memory_space=pl.ANY)],
        out_specs=whole_spec,
        input_output_aliases={4: 0},
        **common,
    )(core, mine, early, late, even)


def gather(value, groups):
    copies = jnp.broadcast_to(value[None], (len(groups[0]),) + value.shape)
    return lax.all_to_all(
        copies.reshape((-1,) + value.shape[1:]), AXES, split_axis=0, concat_axis=0,
        axis_index_groups=groups, tiled=True,
    )


def per_device(pseudo_grad, grad_expo, sign_bits, params, momentum, param_expo):
    owned, width = params.shape
    replicas = lax.axis_size(("zl", "c"))
    me = lax.axis_index(("zl", "c")).astype(jnp.int32)[None]
    table = jnp.asarray(hadamard(width))
    terms, table, params, decayed, own_sign, inverse = encode(
        me, pseudo_grad[0], grad_expo, sign_bits, table, params, momentum, param_expo[None]
    )
    terms = lax.all_to_all(terms, ("zl", "c"), split_axis=0, concat_axis=0, tiled=True)

    total = jnp.sum(terms.reshape(replicas, owned, width).astype(jnp.float32), axis=0)
    delta = jnp.dot(total, table, precision=lax.Precision.HIGHEST) * own_sign
    new_params = params - 0.7 * (delta + 0.9 * (decayed + delta))
    codes = jnp.clip(new_params * inverse, -4.0, 4.0).astype(jnp.bfloat16)
    mine = gather(gather(codes, classes()), cubes())
    mine = mine.reshape(8, 8, 4, owned, width)
    early, late = (
        lax.ppermute(part, "c", [(0, 1), (1, 0)]) for part in (mine[:EARLY], mine[EARLY:])
    )
    core = lax.axis_index("c").astype(jnp.int32)[None]
    whole, new_params, new_momentum = place(
        core, mine, early, owner=(params, decayed, delta)
    )
    whole = place(core, mine, early, late=late, even=whole)
    return new_params, new_momentum, whole.reshape(-1, width)


def solution(mesh):
    names, sizes = zip(*SIZES)
    cut = Mesh(mesh.devices.reshape(sizes), names)
    outer, dev = ("zl", "c"), ("x", "zh", "y")
    owner = dev + outer
    in_specs = (P(outer, dev, None), P(outer, dev), P(dev, None),
                P(owner, None), P(owner, None), P(owner))
    out_specs = (P(owner, None), P(owner, None), P())
    return jax.shard_map(
        per_device, mesh=cut, in_specs=in_specs, out_specs=out_specs, check_vma=False
    )
```

```python
import jax
import jax.numpy as jnp
import numpy as np
from jax import lax
from jax.experimental import pallas as pl
from jax.experimental.pallas import tpu as pltpu
from jax.sharding import Mesh
from jax.sharding import PartitionSpec as P

SIZES = (("zl", 4), ("c", 2), ("x", 4), ("zh", 2), ("y", 8))
AXES = tuple(name for name, _ in SIZES)
BITS = (0, 1)
EARLY = 5


def device(x, y, z, core):
    x, y, z = x % 4, y % 8, z % 8
    return (((z % 4 * 2 + core) * 4 + x) * 2 + z // 4) * 8 + y


def classes():
    return [
        [
            device(row + 2 * z, 2 * yh + (side + z) % 2, z, core)
            for z in range(8)
            for yh in range(4)
        ]
        for row in range(4)
        for side in BITS
        for core in BITS
    ]


def cubes():
    def place_of(chip):
        x, y, z = chip
        row = (x + 2 * z) % 4
        return row % 2, row // 2, (y + z) % 2

    groups = []
    for core, start in enumerate(((0, 0, 1), (1, 1, 0))):
        for x in range(start[0], 4, 2):
            for y in range(start[1], 8, 2):
                for z in range(start[2], 8, 2):
                    cube = [
                        ((x + i) % 4, (y + j) % 8, (z + k) % 8)
                        for i in BITS
                        for j in BITS
                        for k in BITS
                    ]
                    cube.sort(key=place_of)
                    groups.append([device(*chip, core) for chip in cube])
    return groups


def hadamard(width):
    index = np.arange(width)
    common = index[:, None] & index[None, :]
    parity = np.zeros((width, width), np.int32)
    for bit in range(width.bit_length() - 1):
        parity = parity + (common >> bit & 1)
    return (1 - 2 * (parity % 2)).astype(np.float32)


def exact_dot(values, table):
    total = None
    for _ in range(3):
        part = values.astype(jnp.bfloat16)
        values = values - part.astype(jnp.float32)
        product = jnp.dot(part, table, preferred_element_type=jnp.float32)
        total = product if total is None else total + product
    return total


def column(row):
    n = row.shape[1]
    down = lax.broadcasted_iota(jnp.int32, (n, n), 0)
    along = lax.broadcasted_iota(jnp.int32, (n, n), 1)
    spread = jnp.where(down == along, jnp.broadcast_to(row, (n, n)), 0.0)
    return jnp.sum(spread, axis=1, keepdims=True)


def encode_kernel(me_ref, grad_in, expo_in, bits_in, table_in, params_in, momentum_in,
                  param_expo_in, terms_ref, table_ref, params_ref, decayed_ref,
                  own_sign_ref, inverse_ref, grad_ref, expo_ref, bits_ref, momentum_ref,
                  param_expo_ref, sems):
    inward = (
        (grad_in, grad_ref),
        (expo_in, expo_ref),
        (bits_in, bits_ref),
        (table_in, table_ref),
        (params_in, params_ref),
        (momentum_in, momentum_ref),
        (param_expo_in, param_expo_ref),
    )
    copies = [
        pltpu.make_async_copy(source, target, sems.at[i])
        for i, (source, target) in enumerate(inward)
    ]
    for copy in copies:
        copy.start()
    for copy in copies:
        copy.wait()
    width = grad_ref.shape[1]
    owned = own_sign_ref.shape[0]
    replicas = grad_ref.shape[0] // owned
    sign = (2 * bits_ref[...] - 1).astype(jnp.float32)
    table = table_ref[...].astype(jnp.bfloat16)
    rotated = exact_dot(grad_ref[...] * sign, table) * (width**-0.5)
    limit = column(4.0 * jnp.exp2(expo_ref[...].astype(jnp.float32)))
    terms_ref[...] = jnp.clip(rotated, -limit, limit).astype(terms_ref.dtype)
    own = pl.ds(pl.multiple_of(me_ref[0] * owned, owned), owned)
    own_sign = (2 * bits_ref[own, :] - 1).astype(jnp.float32)
    own_sign_ref[...] = own_sign * (width**-0.5 / replicas)
    decayed_ref[...] = 0.9 * momentum_ref[...]
    inverse = column(jnp.exp2(-param_expo_ref[...].astype(jnp.float32)))
    inverse_ref[...] = jnp.broadcast_to(inverse, inverse_ref.shape)


def encode(me, grad, expo, bits, table, params, momentum, param_expo):
    shard, width = grad.shape
    owned = params.shape[0]
    f32 = jnp.float32
    smem = pl.BlockSpec(memory_space=pltpu.SMEM)
    vmem = pl.BlockSpec(memory_space=pltpu.VMEM)
    hbm = pl.BlockSpec(memory_space=pltpu.HBM)
    return pl.pallas_call(
        encode_kernel,
        out_shape=(
            jax.ShapeDtypeStruct((shard, width), jnp.bfloat16),
            jax.ShapeDtypeStruct((width, width), f32),
            jax.ShapeDtypeStruct((owned, width), f32),
            jax.ShapeDtypeStruct((owned, width), f32),
            jax.ShapeDtypeStruct((owned, width), f32),
            jax.ShapeDtypeStruct((owned, width), f32),
        ),
        in_specs=[smem] + [hbm] * 7,
        out_specs=(vmem,) * 6,
        scratch_shapes=[
            pltpu.VMEM((shard, width), f32),
            pltpu.VMEM((1, shard), jnp.int32),
            pltpu.VMEM((shard, width), jnp.int32),
            pltpu.VMEM((owned, width), f32),
            pltpu.VMEM((1, owned), jnp.int32),
            pltpu.SemaphoreType.DMA((7,)),
        ],
        compiler_params=pltpu.CompilerParams(vmem_limit_bytes=4 * 2**20),
    )(
        me,
        *(
            pltpu.with_memory_space_constraint(value, pltpu.HBM)
            for value in (grad, expo, bits, table, params, momentum, param_expo)
        ),
    )


def fill(core_ref, mine, other, out_ref):
    core = core_ref[0]
    for xh in BITS:
        for side, part in ((core, mine), (1 - core, other)):
            for zl in range(4):
                for py in BITS:
                    for zh in BITS:
                        out_ref[xh, 0, zh, :, py, zl, side] = part(
                            (xh + zl) % 2, (py + zl) % 2
                        )[4 * zh + zl]


def place_even_kernel(core_ref, mine_ref, other_ref, params_ref, decayed_ref, delta_ref,
                      out_ref, new_params_ref, new_momentum_ref):
    fill(
        core_ref,
        lambda half, side: mine_ref.at[2 * half + side],
        lambda half, side: other_ref.at[2 * half + side],
        out_ref,
    )
    delta = delta_ref[...]
    new_momentum = decayed_ref[...] + delta
    new_momentum_ref[...] = new_momentum
    new_params_ref[...] = params_ref[...] - 0.7 * (delta + 0.9 * new_momentum)


def place_odd_kernel(core_ref, mine_ref, early_ref, late_ref, even_ref, out_ref):
    early = early_ref.shape[0]

    def other(half, side):
        at = 4 + 2 * half + side
        return early_ref.at[at] if at < early else late_ref.at[at - early]

    fill(core_ref, lambda half, side: mine_ref.at[4 + 2 * half + side], other, out_ref)


def place(core, mine, early, owner=None, late=None, even=None):
    owned, width = mine.shape[-2:]
    px = 0 if even is None else 1
    block = (2, 4, 2, 4, 2, owned, width)
    smem = pl.BlockSpec(memory_space=pltpu.SMEM)
    vmem = pl.BlockSpec(memory_space=pltpu.VMEM)
    whole = jax.ShapeDtypeStruct((2, 2) + block, mine.dtype)
    whole_spec = pl.BlockSpec((2, 1) + block, lambda i: (0, px) + (0,) * len(block))
    small = jax.ShapeDtypeStruct((owned, width), jnp.float32)
    small_spec = pl.BlockSpec((owned, width), lambda i: (0, 0))
    common = dict(
        grid=(1,),
        cost_estimate=pl.CostEstimate(
            flops=0, bytes_accessed=4 * mine.size, transcendentals=0
        ),
        compiler_params=pltpu.CompilerParams(vmem_limit_bytes=16 * 2**20),
    )
    if even is None:
        return pl.pallas_call(
            place_even_kernel,
            out_shape=(whole, small, small),
            in_specs=[smem] + [vmem] * 5,
            out_specs=(whole_spec, small_spec, small_spec),
            **common,
        )(core, mine, early, *owner)
    return pl.pallas_call(
        place_odd_kernel,
        out_shape=whole,
        in_specs=[smem, vmem, vmem, vmem, pl.BlockSpec(memory_space=pl.ANY)],
        out_specs=whole_spec,
        input_output_aliases={4: 0},
        **common,
    )(core, mine, early, late, even)


def gather(value, groups):
    copies = jnp.broadcast_to(value[None], (len(groups[0]),) + value.shape)
    return lax.all_to_all(
        copies.reshape((-1,) + value.shape[1:]), AXES, split_axis=0, concat_axis=0,
        axis_index_groups=groups, tiled=True,
    )


def per_device(pseudo_grad, grad_expo, sign_bits, params, momentum, param_expo):
    owned, width = params.shape
    replicas = lax.axis_size(("zl", "c"))
    me = lax.axis_index(("zl", "c")).astype(jnp.int32)[None]
    table = jnp.asarray(hadamard(width))
    terms, table, params, decayed, own_sign, inverse = encode(
        me, pseudo_grad[0], grad_expo, sign_bits, table, params, momentum, param_expo[None]
    )
    terms = lax.all_to_all(terms, ("zl", "c"), split_axis=0, concat_axis=0, tiled=True)

    total = jnp.sum(terms.reshape(replicas, owned, width).astype(jnp.float32), axis=0)
    delta = jnp.dot(total, table, precision=lax.Precision.HIGHEST) * own_sign
    new_params = params - 0.7 * (delta + 0.9 * (decayed + delta))
    codes = jnp.clip(new_params * inverse, -4.0, 4.0).astype(jnp.bfloat16)
    mine = gather(gather(codes, classes()), cubes())
    mine = mine.reshape(8, 8, 4, owned, width)
    early, late = (
        lax.ppermute(part, "c", [(0, 1), (1, 0)]) for part in (mine[:EARLY], mine[EARLY:])
    )
    core = lax.axis_index("c").astype(jnp.int32)[None]
    whole, new_params, new_momentum = place(
        core, mine, early, owner=(params, decayed, delta)
    )
    whole = place(core, mine, early, late=late, even=whole)
    return new_params, new_momentum, whole.reshape(-1, width)


def solution(mesh):
    names, sizes = zip(*SIZES)
    cut = Mesh(mesh.devices.reshape(sizes), names)
    outer, dev = ("zl", "c"), ("x", "zh", "y")
    owner = dev + outer
    in_specs = (P(outer, dev, None), P(outer, dev), P(dev, None),
                P(owner, None), P(owner, None), P(owner))
    out_specs = (P(owner, None), P(owner, None), P())
    return jax.shard_map(
        per_device, mesh=cut, in_specs=in_specs, out_specs=out_specs, check_vma=False
    )
```
